32 devices in a mesh: dp: 2 (over x), context: 4 (over y, core), tensor: 4 (over z).
Axes of the slice: x: 2, y: 2, z: 4, core: 2. Of those that a mesh axis runs over, the one named last changes fastest.
Arguments:
- tokens: bfloat16 [2, 2048, 5376], P('dp', ('context', 'tensor')), may hold values from -48 to 48
- output_gradient: bfloat16 [2, 2048, 5376], P('dp', ('context', 'tensor')), may hold values from -48 to 48
- document_index: int32 [2, 2048], P('dp'), may hold values from 0 to 3, never falling along the last dimension, each value on 1 to 1024 neighbouring positions
- query_weight: bfloat16 [5376, 4096], P(None, 'tensor'), may hold values from -1 to 1
- key_value_weight: bfloat16 [2, 5376, 2048], P(None, None, 'tensor'), may hold values from -1 to 1
- output_weight: bfloat16 [4096, 5376], P('tensor'), may hold values from -0.09375 to 0.09375
- adapter_down_projections: bfloat16 [3, 16, 5376], replicated, may hold values from -0.078125 to 0.078125
- adapter_up_query: bfloat16 [16, 4096], P(None, 'tensor'), may hold values from -0.29882812 to 0.29882812
- adapter_up_key_value: bfloat16 [2, 16, 2048], P(None, None, 'tensor'), may hold values from -0.29882812 to 0.29882812
- adapter_down_output: bfloat16 [16, 4096], P(None, 'tensor'), may hold values from -0.09375 to 0.09375
- adapter_up_output: bfloat16 [16, 5376], replicated, may hold values from -0.29882812 to 0.29882812
Outputs:
- grad_input: bfloat16 [2, 2048, 5376], P('dp', ('context', 'tensor'))
- grad_down_qkv: float32 [3, 16, 5376], replicated
- query_up_gradient: float32 [16, 4096], P(None, 'tensor')
- grad_up_keyvalue: float32 [2, 16, 2048], P(None, None, 'tensor')
- grad_down_out: float32 [16, 4096], P(None, 'tensor')
- output_up_gradient: float32 [16, 5376], replicated
The draws below stay inside these ranges and needn't reach their ends.
Inputs may be any that keep to these rules, and one draw needn't show every extreme that they name: `document_index`: ids never fall along a sequence; each document holds 1 to half of 2048 tokens, and one holds exactly that many.
All inputs are finite; a program needn't handle non-finite values.
Results may differ from the reference program's by a relative error of at most 0.03.
Values may be sent and summed in bfloat16 or wider, within the bound.
A program may use at most 192 MiB of HBM per device.

```python
import math
import jax
import jax.numpy as jnp
import numpy as np
from jax import lax

MODEL_DIM = 5376
QUERY_HEADS = 32
KEY_VALUE_HEADS = 16
HEAD_SIZE = 128
WINDOW = 1024
ADAPTER_RANK = 16
CTX_TOK = 512
SEQUENCE_TOKENS = 2048
SEQS = 2
HALO = 2
N_CONTEXT = 4
N_TENSOR = 4


def projection_tables(key):
    common_term = jax.random.truncated_normal(jax.random.fold_in(key, 11), -6.0, 6.0, (2, MODEL_DIM, KEY_VALUE_HEADS, HEAD_SIZE), jnp.float32)
    self_term = jax.random.truncated_normal(jax.random.fold_in(key, 12), -6.0, 6.0, (MODEL_DIM, KEY_VALUE_HEADS, QUERY_HEADS // KEY_VALUE_HEADS, HEAD_SIZE), jnp.float32)
    query_table = self_term
    query_table = query_table.reshape(MODEL_DIM, QUERY_HEADS * HEAD_SIZE) * MODEL_DIM ** (-0.5)
    key_value_matrix = common_term.reshape(2, MODEL_DIM, KEY_VALUE_HEADS * HEAD_SIZE) * MODEL_DIM ** (-0.5)
    return (jnp.clip(query_table, -1.0, 1.0), jnp.clip(key_value_matrix, -1.0, 1.0))


def draw_query_weight(key, part):
    return projection_tables(key)[0].astype(jnp.bfloat16)


def draw_key_value_weight(key, part):
    return projection_tables(key)[1].astype(jnp.bfloat16)


def draw_tokens(key, part):
    sample = jax.random.truncated_normal(jax.random.fold_in(key, 21), -6.0, 6.0, (SEQS, SEQUENCE_TOKENS, MODEL_DIM), jnp.float32)
    return jnp.clip(sample, -48.0, 48.0).astype(jnp.bfloat16)


def block_scale(key, extent, shards, smallest, top_value):
    loudness = 1.0
    for axis_at, blocks in shards:
        heights = jax.random.uniform(jax.random.fold_in(jax.random.fold_in(key, 6), axis_at), (blocks,), jnp.float32, smallest / len(shards), top_value / len(shards))
        loudness = loudness * jnp.repeat(jnp.exp(heights), extent[axis_at] // blocks).reshape((-1,) + (1,) * (len(extent) - 1 - axis_at))
    return loudness


def profile(number_of, total, reach, slope):
    loads = [(1 << 20) // math.isqrt(standing ** slope) + 1 for standing in range(2, number_of + 1)]
    surplus, holding = total - reach - (number_of - 1), [1] * (number_of - 1)
    while surplus > 0:
        free = [i for i in range(number_of - 1) if holding[i] < reach]
        whole, remaining = sum([loads[i] for i in free]), surplus
        for i in free:
            addition = min(reach - holding[i], max(1, remaining * loads[i] // whole), surplus)
            holding[i] = holding[i] + addition
            surplus = surplus - addition
    return np.array([reach] + holding)


def uneven(stream_key, amount, total, bound, slope):
    if amount == 2:
        one = jax.random.randint(stream_key, (), max(1, total - bound), min(bound, total - 1) + 1)
        return jnp.stack([one, total - one])
    tallies = jnp.asarray(profile(amount, total, bound, slope), jnp.int32)
    pairs = (amount - 1) // 2
    donor, receiver = tallies[1:1 + 2 * pairs:2], tallies[2:2 + 2 * pairs:2]
    margin = jnp.minimum(donor - 1, bound - receiver)
    shifted = jax.random.randint(jax.random.fold_in(stream_key, 1), (pairs,), 0, 1 << 20) % (margin + 1)
    tallies = tallies.at[1:1 + 2 * pairs:2].set(donor - shifted).at[2:2 + 2 * pairs:2].set(receiver + shifted)
    return tallies[jax.random.permutation(jax.random.fold_in(stream_key, 2), amount)]


def scatter_about(stream_key, extent, spread, bound, split=(), kind=jnp.bfloat16):
    array = jax.random.normal(stream_key, extent, jnp.float32) * spread
    if len(split) > 0:
        array = block_scale(stream_key, extent, split, -0.22, 0.18) * array
    return jnp.clip(array, min=-bound, max=bound).astype(kind)


def setup_inputs(seed: int = 0) -> dict:
    seeds = jax.random.split(jax.random.key(seed), 12)
    tokens = draw_tokens(jax.random.fold_in(seeds[11], 71), 0)
    output_gradient = scatter_about(seeds[1], (SEQS, SEQUENCE_TOKENS, MODEL_DIM), 8.0, 48.0, ((0, 2), (1, 16)))
    document_index = jax.vmap(lambda own: jnp.searchsorted(jnp.cumsum(uneven(own, 4, SEQUENCE_TOKENS, SEQUENCE_TOKENS // 2, 1)), jnp.arange(SEQUENCE_TOKENS), side="right"))(jax.random.split(seeds[2], SEQS)).reshape((SEQS, SEQUENCE_TOKENS)).astype(jnp.int32)
    query_weight = draw_query_weight(jax.random.fold_in(seeds[11], 71), 0)
    key_value_weight = draw_key_value_weight(jax.random.fold_in(seeds[11], 71), 0)
    output_weight = scatter_about(seeds[5], (QUERY_HEADS * HEAD_SIZE, MODEL_DIM), (QUERY_HEADS * HEAD_SIZE) ** -0.5, 0.09375, ((0, 4),))
    adapter_down_projections = scatter_about(seeds[6], (3, ADAPTER_RANK, MODEL_DIM), MODEL_DIM ** -0.5, 0.078125)
    adapter_up_query = scatter_about(seeds[7], (ADAPTER_RANK, QUERY_HEADS * HEAD_SIZE), 0.05, 0.29882812, ((1, 4),))
    adapter_up_key_value = scatter_about(seeds[8], (2, ADAPTER_RANK, KEY_VALUE_HEADS * HEAD_SIZE), 0.05, 0.29882812, ((2, 4),))
    adapter_down_output = scatter_about(seeds[9], (ADAPTER_RANK, QUERY_HEADS * HEAD_SIZE), (QUERY_HEADS * HEAD_SIZE) ** -0.5, 0.09375, ((1, 4),))
    adapter_up_output = scatter_about(seeds[10], (ADAPTER_RANK, MODEL_DIM), 0.05, 0.29882812)
    return {"tokens": tokens, "output_gradient": output_gradient, "document_index": document_index, "query_weight": query_weight, "key_value_weight": key_value_weight, "output_weight": output_weight, "adapter_down_projections": adapter_down_projections, "adapter_up_query": adapter_up_query, "adapter_up_key_value": adapter_up_key_value, "adapter_down_output": adapter_down_output, "adapter_up_output": adapter_up_output}


adapter_scale = 2.0
attn_scale = 168.0 ** -0.5
rope_base = 10000.0


def rope_tables(positions, head_width):
    half_width = head_width // 2
    inverse = rope_base ** (-(jnp.arange(half_width, dtype=jnp.float32) * 2.0 / head_width))
    angle = positions[:, None] * inverse[None, :]
    return jnp.cos(angle), jnp.sin(angle)


def apply_rotation(vectors, cosine_table, sine_values):
    half_width = vectors.shape[-1] // 2
    front_half = vectors[..., :half_width]
    back_half = vectors[..., half_width:]
    cosine_table = cosine_table[:, None, :]
    sine_values = sine_values[:, None, :]
    return jnp.concatenate([front_half * cosine_table - back_half * sine_values, back_half * cosine_table + front_half * sine_values], -1)


def undo_rotation(grads, cosine_table, sine_values):
    half_width = grads.shape[-1] // 2
    front_half = grads[..., :half_width]
    back_half = grads[..., half_width:]
    cosine_table = cosine_table[:, None, :]
    sine_values = sine_values[:, None, :]
    return jnp.concatenate([front_half * cosine_table + back_half * sine_values, back_half * cosine_table - front_half * sine_values], -1)


def to_low(values_high):
    return lax.optimization_barrier(values_high.astype(jnp.bfloat16)).astype(jnp.float32)


def band_block(queries, key_rows, value_rows, attention_output_gradient, allowed):
    row_count, heads_q, head_width = queries.shape
    heads_kv = key_rows.shape[1]
    group_size = heads_q // heads_kv
    query_groups = queries.astype(jnp.float32).reshape(row_count, heads_kv, group_size, head_width)
    grad_groups = attention_output_gradient.astype(jnp.float32).reshape(row_count, heads_kv, group_size, head_width)
    key_high = key_rows.astype(jnp.float32)
    value_high = value_rows.astype(jnp.float32)
    scores = jnp.einsum("chgd,khd->hgck", query_groups, key_high) * attn_scale
    scores = jnp.where(allowed[None, None], scores, -1e30)
    row_max = jnp.max(scores, -1, keepdims=True)
    exponent = jnp.exp(scores - row_max)
    weights = exponent / jnp.sum(exponent, -1, keepdims=True)
    weights_low = to_low(weights)
    attention_output = to_low(jnp.einsum("hgck,khd->chgd", weights_low, value_high))
    grad_weights = jnp.einsum("chgd,khd->hgck", grad_groups, value_high)
    row_dot = jnp.einsum("chgd,chgd->hgc", grad_groups, attention_output)
    grad_scores = to_low(weights * (grad_weights - row_dot[..., None]) * attn_scale)
    query_gradient = jnp.einsum("hgck,khd->chgd", grad_scores, key_high)
    key_gradient = jnp.einsum("hgck,chgd->khd", grad_scores, query_groups)
    value_gradient = jnp.einsum("hgck,chgd->khd", weights_low, grad_groups)
    return (attention_output.astype(jnp.bfloat16).reshape(row_count, heads_q, head_width),
            query_gradient.reshape(row_count, heads_q, head_width), key_gradient, value_gradient)


def reference(tokens, output_gradient, document_index, query_weight, key_value_weight, output_weight, adapter_down_projections, adapter_up_query, adapter_up_key_value, adapter_down_output, adapter_up_output):
    shard_len = CTX_TOK
    padding_length = HALO * shard_len
    query_columns = QUERY_HEADS * HEAD_SIZE // N_TENSOR
    key_value_columns = KEY_VALUE_HEADS * HEAD_SIZE // N_TENSOR
    down_factors_all = adapter_down_projections.reshape(3 * ADAPTER_RANK, MODEL_DIM)
    cosine_table, sine_values = rope_tables(jnp.arange(SEQUENCE_TOKENS).astype(jnp.float32), HEAD_SIZE)
    outputs = []
    grad_down_total = jnp.zeros((3 * ADAPTER_RANK, MODEL_DIM), jnp.float32)
    query_up_gradient = jnp.zeros((ADAPTER_RANK, QUERY_HEADS * HEAD_SIZE), jnp.float32)
    key_up_gradient = jnp.zeros((ADAPTER_RANK, KEY_VALUE_HEADS * HEAD_SIZE), jnp.float32)
    value_up_gradient = jnp.zeros((ADAPTER_RANK, KEY_VALUE_HEADS * HEAD_SIZE), jnp.float32)
    grad_down_out = jnp.zeros((ADAPTER_RANK, QUERY_HEADS * HEAD_SIZE), jnp.float32)
    output_up_gradient = jnp.zeros((ADAPTER_RANK, MODEL_DIM), jnp.float32)
    for sequence in range(SEQS):
        input_tokens = tokens[sequence]
        incoming_gradient = output_gradient[sequence]
        segment_row = document_index[sequence]
        adapted = jnp.dot(input_tokens, down_factors_all.T, preferred_element_type=jnp.float32).astype(jnp.bfloat16)
        adapted_query = adapted[:, :ADAPTER_RANK]
        adapted_key = adapted[:, ADAPTER_RANK:2 * ADAPTER_RANK]
        adapted_value = adapted[:, 2 * ADAPTER_RANK:]
        query_linear = jnp.dot(input_tokens, query_weight, preferred_element_type=jnp.float32) + adapter_scale * jnp.dot(adapted_query, adapter_up_query, preferred_element_type=jnp.float32)
        key_linear = jnp.dot(input_tokens, key_value_weight[0], preferred_element_type=jnp.float32) + adapter_scale * jnp.dot(adapted_key, adapter_up_key_value[0], preferred_element_type=jnp.float32)
        value_linear = jnp.dot(input_tokens, key_value_weight[1], preferred_element_type=jnp.float32) + adapter_scale * jnp.dot(adapted_value, adapter_up_key_value[1], preferred_element_type=jnp.float32)
        queries = apply_rotation(query_linear.reshape(SEQUENCE_TOKENS, QUERY_HEADS, HEAD_SIZE), cosine_table, sine_values).astype(jnp.bfloat16)
        key_full = apply_rotation(key_linear.reshape(SEQUENCE_TOKENS, KEY_VALUE_HEADS, HEAD_SIZE), cosine_table, sine_values).astype(jnp.bfloat16)
        value_full = value_linear.reshape(SEQUENCE_TOKENS, KEY_VALUE_HEADS, HEAD_SIZE).astype(jnp.bfloat16)
        up_gradient = (adapter_scale * jnp.dot(incoming_gradient, adapter_up_output.T, preferred_element_type=jnp.float32)).astype(jnp.bfloat16)
        attention_output_gradient = (jnp.dot(incoming_gradient, output_weight.T, preferred_element_type=jnp.float32) + jnp.dot(up_gradient, adapter_down_output, preferred_element_type=jnp.float32)).astype(jnp.bfloat16)
        attention_output_gradient = attention_output_gradient.reshape(SEQUENCE_TOKENS, QUERY_HEADS, HEAD_SIZE)
        key_padded = jnp.concatenate([jnp.zeros((padding_length, KEY_VALUE_HEADS, HEAD_SIZE), jnp.bfloat16), key_full], 0)
        value_padded = jnp.concatenate([jnp.zeros((padding_length, KEY_VALUE_HEADS, HEAD_SIZE), jnp.bfloat16), value_full], 0)
        segment_pad = jnp.concatenate([jnp.full((padding_length,), -1, jnp.int32), segment_row.astype(jnp.int32)], 0)

        def one_block(block_at):
            begin_at = (block_at * shard_len).astype(jnp.int32)
            query_part = lax.dynamic_slice_in_dim(queries, begin_at, shard_len, 0)
            grad_part = lax.dynamic_slice_in_dim(attention_output_gradient, begin_at, shard_len, 0)
            key_part = lax.dynamic_slice_in_dim(key_padded, begin_at, padding_length + shard_len, 0)
            value_part = lax.dynamic_slice_in_dim(value_padded, begin_at, padding_length + shard_len, 0)
            key_seg = lax.dynamic_slice_in_dim(segment_pad, begin_at, padding_length + shard_len, 0)
            query_seg = lax.dynamic_slice_in_dim(segment_row.astype(jnp.int32), begin_at, shard_len, 0)
            query_pos = begin_at + jnp.arange(shard_len, dtype=jnp.int32)
            key_pos = begin_at - padding_length + jnp.arange(padding_length + shard_len, dtype=jnp.int32)
            offset = query_pos[:, None] - key_pos[None, :]
            allowed = (key_pos >= 0)[None, :] & (offset >= 0) & (offset < WINDOW) & (query_seg[:, None] == key_seg[None, :])
            return band_block(query_part, key_part, value_part, grad_part, allowed)

        attention_output, grad_query_rot, grad_key_parts, grad_value_parts = lax.map(one_block, jnp.arange(N_CONTEXT, dtype=jnp.int32))
        pair_parts = jnp.stack([grad_key_parts, grad_value_parts], 1)

        def extra_term(block_at, running):
            begin_at = (block_at * shard_len).astype(jnp.int32)
            current = lax.dynamic_slice_in_dim(running, begin_at, padding_length + shard_len, 1)
            return lax.dynamic_update_slice_in_dim(running, current + pair_parts[block_at], begin_at, 1)

        pairwise_total = lax.fori_loop(0, N_CONTEXT, extra_term, jnp.zeros((2, padding_length + SEQUENCE_TOKENS, KEY_VALUE_HEADS, HEAD_SIZE), jnp.float32))
        pairwise_total = pairwise_total[:, padding_length:]
        attention_output = attention_output.reshape(SEQUENCE_TOKENS, QUERY_HEADS * HEAD_SIZE)
        query_gradient = undo_rotation(grad_query_rot.reshape(SEQUENCE_TOKENS, QUERY_HEADS, HEAD_SIZE), cosine_table, sine_values).reshape(SEQUENCE_TOKENS, QUERY_HEADS * HEAD_SIZE).astype(jnp.bfloat16)
        key_gradient = undo_rotation(pairwise_total[0], cosine_table, sine_values).reshape(SEQUENCE_TOKENS, KEY_VALUE_HEADS * HEAD_SIZE).astype(jnp.bfloat16)
        value_gradient = pairwise_total[1].reshape(SEQUENCE_TOKENS, KEY_VALUE_HEADS * HEAD_SIZE).astype(jnp.bfloat16)
        factor_value = jnp.dot(attention_output, adapter_down_output.T, preferred_element_type=jnp.float32).astype(jnp.bfloat16)
        output_up_gradient = output_up_gradient + adapter_scale * jnp.dot(factor_value.T, incoming_gradient, preferred_element_type=jnp.float32)
        grad_down_out = grad_down_out + jnp.dot(up_gradient.T, attention_output, preferred_element_type=jnp.float32)
        query_up_gradient = query_up_gradient + adapter_scale * jnp.dot(adapted_query.T, query_gradient, preferred_element_type=jnp.float32)
        key_up_gradient = key_up_gradient + adapter_scale * jnp.dot(adapted_key.T, key_gradient, preferred_element_type=jnp.float32)
        value_up_gradient = value_up_gradient + adapter_scale * jnp.dot(adapted_value.T, value_gradient, preferred_element_type=jnp.float32)
        input_total = jnp.zeros((SEQUENCE_TOKENS, MODEL_DIM), jnp.float32)
        for group_index in range(N_TENSOR):
            query_lowrank = group_index * query_columns
            key_value_lowrank = group_index * key_value_columns
            query_gradient_grouped = query_gradient[:, query_lowrank:query_lowrank + query_columns]
            key_gradient_grouped = key_gradient[:, key_value_lowrank:key_value_lowrank + key_value_columns]
            value_gradient_grouped = value_gradient[:, key_value_lowrank:key_value_lowrank + key_value_columns]
            query_hidden = (adapter_scale * jnp.dot(query_gradient_grouped, adapter_up_query[:, query_lowrank:query_lowrank + query_columns].T, preferred_element_type=jnp.float32)).astype(jnp.bfloat16)
            key_hidden = (adapter_scale * jnp.dot(key_gradient_grouped, adapter_up_key_value[0][:, key_value_lowrank:key_value_lowrank + key_value_columns].T, preferred_element_type=jnp.float32)).astype(jnp.bfloat16)
            value_hidden = (adapter_scale * jnp.dot(value_gradient_grouped, adapter_up_key_value[1][:, key_value_lowrank:key_value_lowrank + key_value_columns].T, preferred_element_type=jnp.float32)).astype(jnp.bfloat16)
            hidden_all = jnp.concatenate([query_hidden, key_hidden, value_hidden], 1)
            grad_down_total = grad_down_total + jnp.dot(hidden_all.T, input_tokens, preferred_element_type=jnp.float32)
            term = jnp.dot(query_gradient_grouped, query_weight[:, query_lowrank:query_lowrank + query_columns].T, preferred_element_type=jnp.float32)
            term = term + jnp.dot(key_gradient_grouped, key_value_weight[0][:, key_value_lowrank:key_value_lowrank + key_value_columns].T, preferred_element_type=jnp.float32)
            term = term + jnp.dot(value_gradient_grouped, key_value_weight[1][:, key_value_lowrank:key_value_lowrank + key_value_columns].T, preferred_element_type=jnp.float32)
            term = term + jnp.dot(hidden_all, down_factors_all, preferred_element_type=jnp.float32)
            input_total = input_total + to_low(term)
        outputs.append(input_total.astype(jnp.bfloat16))
    grad_input = jnp.stack(outputs, 0)
    return (grad_input, grad_down_total.reshape(3, ADAPTER_RANK, MODEL_DIM), query_up_gradient,
            jnp.stack([key_up_gradient, value_up_gradient], 0), grad_down_out, output_up_gradient)
```

```python
import functools

import jax
import jax.numpy as jnp
from jax import lax
from jax.experimental import pallas as pl
from jax.experimental.pallas import tpu as pltpu
from jax.sharding import PartitionSpec as P

HEAD_SIZE = 128
WINDOW = 1024


adapter_scale = 2.0
attn_scale = 168.0 ** (-0.5)
rope_base = 10000.0


def passed_along(block, axis, distance):
    devices = range(lax.axis_size(axis))
    route = [(i - distance, i) for i in devices if i - distance in devices]
    return lax.ppermute(block, axis, route)


def rope_tables(positions, head_width):
    half_width = head_width // 2
    inverse = rope_base ** (-(jnp.arange(half_width, dtype=jnp.float32) * 2.0 / head_width))
    angle = positions[:, None] * inverse[None, :]
    return (jnp.cos(angle), jnp.sin(angle))


NT = (((1,), (1,)), ((), ()))
TN = (((0,), (0,)), ((), ()))
f32 = jnp.float32
bf16 = jnp.bfloat16


def dot(a, b, dims):
    return lax.dot_general(a, b, dims, preferred_element_type=f32)


def turned(x, cosine, sine):
    return x * cosine + pltpu.roll(x, x.shape[-1] // 2, 1) * sine


def rope_query_kernel(x_ref, cos_ref, sin_ref, out_ref):
    out_ref[...] = turned(x_ref[...], cos_ref[...], sin_ref[...]).astype(bf16)


def rope_pair_kernel(k_ref, v_ref, cos_ref, sin_ref, out_ref):
    out_ref[0] = turned(k_ref[...], cos_ref[...], sin_ref[...]).astype(bf16)
    out_ref[1] = v_ref[...].astype(bf16)


def rope_query(x, cosine, sine):
    rows, cols = x.shape
    table = pl.BlockSpec((rows, HEAD_SIZE), lambda h: (0, 0))
    return pl.pallas_call(
        rope_query_kernel,
        grid=(cols // HEAD_SIZE,),
        in_specs=[pl.BlockSpec((rows, HEAD_SIZE), lambda h: (0, h)), table, table],
        out_specs=pl.BlockSpec((rows, HEAD_SIZE), lambda h: (0, h)),
        out_shape=jax.ShapeDtypeStruct((rows, cols), bf16),
        name="rope_query",
        cost_estimate=pl.CostEstimate(flops=4 * rows * cols, bytes_accessed=6 * rows * cols, transcendentals=0),
    )(x, cosine, sine)


def rope_pair(k, v, cosine, sine):
    rows, cols = k.shape
    table = pl.BlockSpec((rows, HEAD_SIZE), lambda h: (0, 0))
    block = pl.BlockSpec((rows, HEAD_SIZE), lambda h: (0, h))
    return pl.pallas_call(
        rope_pair_kernel,
        grid=(cols // HEAD_SIZE,),
        in_specs=[block, block, table, table],
        out_specs=pl.BlockSpec((2, rows, HEAD_SIZE), lambda h: (0, 0, h)),
        out_shape=jax.ShapeDtypeStruct((2, rows, cols), bf16),
        name="rope_pair",
        cost_estimate=pl.CostEstimate(flops=4 * rows * cols, bytes_accessed=12 * rows * cols, transcendentals=0),
    )(k, v, cosine, sine)


def band(block, rows, halo_rows, keys):
    first = max(0, (halo_rows + block * rows - WINDOW + 1) // 128 * 128)
    return first, min(keys, halo_rows + (block + 1) * rows)


def fill(refs, k_buf, v_buf):
    at = 0
    for ref in refs:
        n = ref.shape[1]
        k_buf[at : at + n] = ref[0]
        v_buf[at : at + n] = ref[1]
        at += n


def forward_kernel(halo_rows, group, rows, *refs):
    q_ref, qseg_ref, kseg_ref = refs[:3]
    pair_refs = refs[3:-5]
    w_ref, att_ref, k_buf, v_buf, bias = refs[-5:]
    keys, count = bias.shape
    fill(pair_refs, k_buf, v_buf)

    @pl.when(pl.program_id(0) == 0)
    def _():
        for b in range(count // rows):
            lo, hi = band(b, rows, halo_rows, keys)
            shape = (hi - lo, rows)
            offset = (
                lax.broadcasted_iota(jnp.int32, shape, 1)
                - lax.broadcasted_iota(jnp.int32, shape, 0)
                + (halo_rows + b * rows - lo)
            )
            same = kseg_ref[lo:hi, :] == qseg_ref[:, b * rows : (b + 1) * rows]
            allowed = same & (offset >= 0) & (offset < WINDOW)
            bias[lo:hi, b * rows : (b + 1) * rows] = jnp.where(allowed, 0.0, -1e30)

    for g in range(group):
        for b in range(count // rows):
            lo, hi = band(b, rows, halo_rows, keys)
            here = slice(b * rows, (b + 1) * rows)
            cols = slice(g * HEAD_SIZE, (g + 1) * HEAD_SIZE)
            s = dot(k_buf[lo:hi], q_ref[here, cols], NT) * attn_scale + bias[lo:hi, here]
            p = jnp.exp(s - jnp.max(s, axis=0, keepdims=True))
            w = (p * (1.0 / jnp.sum(p, axis=0, keepdims=True))).astype(bf16)
            w_ref[g, lo:hi, here] = w
            att_ref[here, cols] = dot(v_buf[lo:hi], w, TN).T.astype(bf16)


def attention_forward(queries, pairs, query_seg, key_seg):
    count, q_cols = queries.shape
    kv_cols = pairs[0].shape[2]
    group = q_cols // kv_cols
    keys = count * len(pairs)
    rows = min(256, count)
    halo_rows = keys - count
    q_spec = pl.BlockSpec((count, group * HEAD_SIZE), lambda h: (0, h))
    pair_spec = pl.BlockSpec((2, count, HEAD_SIZE), lambda h: (0, 0, h))
    return pl.pallas_call(
        functools.partial(forward_kernel, halo_rows, group, rows),
        grid=(kv_cols // HEAD_SIZE,),
        in_specs=[
            q_spec,
            pl.BlockSpec((1, count), lambda h: (0, 0)),
            pl.BlockSpec((keys, 1), lambda h: (0, 0)),
        ]
        + [pair_spec] * len(pairs),
        out_specs=[pl.BlockSpec((group, keys, count), lambda h: (h, 0, 0)), q_spec],
        out_shape=[
            jax.ShapeDtypeStruct((q_cols // HEAD_SIZE, keys, count), bf16),
            jax.ShapeDtypeStruct((count, q_cols), bf16),
        ],
        scratch_shapes=[
            pltpu.VMEM((keys, HEAD_SIZE), bf16),
            pltpu.VMEM((keys, HEAD_SIZE), bf16),
            pltpu.VMEM((keys, count), f32),
        ],
        compiler_params=pltpu.CompilerParams(vmem_limit_bytes=48 << 20),
        name="attention_forward",
        cost_estimate=pl.CostEstimate(
            flops=4 * q_cols * count * keys, bytes_accessed=40 << 20, transcendentals=8 * count * keys
        ),
    )(queries, query_seg, key_seg, *pairs)


def backward_kernel(halo_rows, group, rows, n_pairs, *refs):
    q_ref, g_ref, att_ref, w_ref, cos_ref, sin_ref = refs[:6]
    pair_refs = refs[6 : 6 + n_pairs]
    dq_ref, halo_ref, own_ref, k_buf, v_buf, dk_buf, dv_buf = refs[6 + n_pairs :]
    keys = k_buf.shape[0]
    count = q_ref.shape[0]
    half = HEAD_SIZE // 2
    fill(pair_refs, k_buf, v_buf)
    dk_buf[...] = jnp.zeros_like(dk_buf)
    dv_buf[...] = jnp.zeros_like(dv_buf)
    for b in range(count // rows):
        lo, hi = band(b, rows, halo_rows, keys)
        here = slice(b * rows, (b + 1) * rows)
        for h in range(group):
            cols = slice(h * HEAD_SIZE, (h + 1) * HEAD_SIZE)
            g = g_ref[here, cols]
            w = w_ref[h, lo:hi, here]
            row_dot = jnp.sum((g.astype(f32) * att_ref[here, cols].astype(f32)).T, axis=0, keepdims=True)
            gw = dot(v_buf[lo:hi], g, NT)
            ds = (w.astype(f32) * ((gw - row_dot) * attn_scale)).astype(bf16)
            dv_buf[lo:hi] += dot(w, g, (((1,), (0,)), ((), ())))
            dk_buf[lo:hi] += dot(ds, q_ref[here, cols], (((1,), (0,)), ((), ())))
            dq = dot(k_buf[lo:hi], ds, TN).T
            dq_ref[here, cols] = turned(dq, cos_ref[here], -sin_ref[here]).astype(bf16)
    if halo_rows:
        halo_ref[0] = dk_buf[:halo_rows].astype(bf16)
        halo_ref[1] = dv_buf[:halo_rows].astype(bf16)
    own_ref[0] = dk_buf[halo_rows:]
    own_ref[1] = dv_buf[halo_rows:]


def attention_backward(queries, grads, attended, weights, pairs, cosine, sine):
    count, q_cols = queries.shape
    kv_cols = pairs[0].shape[2]
    group = q_cols // kv_cols
    keys = count * len(pairs)
    rows = min(256, count)
    halo_rows = keys - count
    q_spec = pl.BlockSpec((count, group * HEAD_SIZE), lambda h: (0, h))
    pair_spec = pl.BlockSpec((2, count, HEAD_SIZE), lambda h: (0, 0, h))
    table = pl.BlockSpec((count, HEAD_SIZE), lambda h: (0, 0))
    return pl.pallas_call(
        functools.partial(backward_kernel, halo_rows, group, rows, len(pairs)),
        grid=(kv_cols // HEAD_SIZE,),
        in_specs=[
            q_spec,
            q_spec,
            q_spec,
            pl.BlockSpec((group, keys, count), lambda h: (h, 0, 0)),
            table,
            table,
        ]
        + [pair_spec] * len(pairs),
        out_specs=[
            q_spec,
            pl.BlockSpec((2, halo_rows, HEAD_SIZE), lambda h: (0, 0, h)),
            pair_spec,
        ],
        out_shape=[
            jax.ShapeDtypeStruct((count, q_cols), bf16),
            jax.ShapeDtypeStruct((2, halo_rows, kv_cols), bf16),
            jax.ShapeDtypeStruct((2, count, kv_cols), f32),
        ],
        scratch_shapes=[
            pltpu.VMEM((keys, HEAD_SIZE), bf16),
            pltpu.VMEM((keys, HEAD_SIZE), bf16),
            pltpu.VMEM((keys, HEAD_SIZE), f32),
            pltpu.VMEM((keys, HEAD_SIZE), f32),
        ],
        compiler_params=pltpu.CompilerParams(vmem_limit_bytes=48 << 20),
        name="attention_backward",
        cost_estimate=pl.CostEstimate(
            flops=8 * q_cols * count * keys, bytes_accessed=20 << 20, transcendentals=0
        ),
    )(queries, grads, attended, weights, cosine, sine, *pairs)


def combine_kernel(own_ref, cos_ref, sin_ref, *refs):
    dk_ref, dv_ref = refs[-2:]
    dk, dv = own_ref[0], own_ref[1]
    for ref in refs[:-2]:
        dk = dk + ref[0].astype(f32)
        dv = dv + ref[1].astype(f32)
    dk_ref[...] = turned(dk, cos_ref[...], -sin_ref[...]).astype(bf16)
    dv_ref[...] = dv.astype(bf16)


def combine(own, shares, cosine, sine):
    _, count, kv_cols = own.shape
    pair_spec = pl.BlockSpec((2, count, HEAD_SIZE), lambda h: (0, 0, h))
    table = pl.BlockSpec((count, HEAD_SIZE), lambda h: (0, 0))
    out = pl.BlockSpec((count, HEAD_SIZE), lambda h: (0, h))
    return pl.pallas_call(
        combine_kernel,
        grid=(kv_cols // HEAD_SIZE,),
        in_specs=[pair_spec, table, table] + [pair_spec] * len(shares),
        out_specs=[out, out],
        out_shape=[jax.ShapeDtypeStruct((count, kv_cols), bf16)] * 2,
        name="combine_pairs",
        cost_estimate=pl.CostEstimate(flops=8 * count * kv_cols, bytes_accessed=20 * count * kv_cols, transcendentals=0),
    )(own, cosine, sine, *shares)


def term_kernel(first_ref, dk_ref, dv_ref, hid_ref, kv_ref, down_ref, out_ref):
    total = first_ref[...] + dot(dk_ref[...], kv_ref[0], NT)
    total = total + dot(dv_ref[...], kv_ref[1], NT)
    total = total + dot(hid_ref[...], down_ref[...], (((1,), (0,)), ((), ())))
    out_ref[...] = total.astype(bf16)


def term_sum(first, dk, dv, hidden, kv_weight, down):
    count, width = first.shape
    tile = next(t for t in (768, 384, 256, 128, width) if width % t == 0)
    whole = lambda a: pl.BlockSpec(a.shape, lambda i: (0, 0))
    block = pl.BlockSpec((count, tile), lambda i: (0, i))
    return pl.pallas_call(
        term_kernel,
        grid=(width // tile,),
        in_specs=[
            block,
            whole(dk),
            whole(dv),
            whole(hidden),
            pl.BlockSpec((2, tile, kv_weight.shape[2]), lambda i: (0, i, 0)),
            pl.BlockSpec((down.shape[0], tile), lambda i: (0, i)),
        ],
        out_specs=block,
        out_shape=jax.ShapeDtypeStruct((count, width), bf16),
        compiler_params=pltpu.CompilerParams(vmem_limit_bytes=48 << 20),
        name="input_term",
        cost_estimate=pl.CostEstimate(
            flops=4 * count * width * dk.shape[1], bytes_accessed=28 << 20, transcendentals=0
        ),
    )(first, dk, dv, hidden, kv_weight, down)


def shifted(block, axis, distance):
    n = lax.axis_size(axis)
    return lax.ppermute(block, axis, [(i, (i + distance) % n) for i in range(n)])


def summed_pairwise(block, axis):
    n = lax.axis_size(axis)
    if n & (n - 1):
        return lax.psum(block, axis)
    step = 1
    while step < n:
        other = lax.ppermute(block, axis, [(i, i ^ step) for i in range(n)])
        block = (block.astype(f32) + other.astype(f32)).astype(bf16)
        step *= 2
    return block


def scattered_rows(block, axis):
    n, me = lax.axis_size(axis), lax.axis_index(axis)
    blocks = block.reshape(n, block.shape[0] // n, block.shape[1])
    total = lax.dynamic_index_in_dim(blocks, me, 0, keepdims=False).astype(f32)
    for d in range(1, n):
        part = lax.dynamic_index_in_dim(blocks, (me + d) % n, 0, keepdims=False)
        total = total + shifted(part, axis, d).astype(f32)
    return total


def gathered_rows(block, axis):
    n, me = lax.axis_size(axis), lax.axis_index(axis)
    parts = jnp.stack([block] + [shifted(block, axis, d) for d in range(1, n)], 0)
    order = (me - jnp.arange(n)) % n
    return jnp.take(parts, order, axis=0).reshape(n * block.shape[0], block.shape[1])


def local(
    tokens,
    output_gradient,
    document_index,
    query_weight,
    key_value_weight,
    output_weight,
    adapter_down_projections,
    adapter_up_query,
    adapter_up_key_value,
    adapter_down_output,
    adapter_up_output,
):
    tensor_size = lax.axis_size("tensor")
    context_at = lax.axis_index("context")
    local_count = tokens.shape[1]
    width = tokens.shape[2]
    shard_len = local_count * tensor_size
    halo_count = (WINDOW - 1) // shard_len + 1
    rank = adapter_down_projections.shape[1]
    gathered = lax.all_gather(tokens[0], "tensor", axis=0, tiled=True)
    incoming = lax.all_gather(output_gradient[0], "tensor", axis=0, tiled=True)
    positions = (context_at * shard_len + jnp.arange(shard_len, dtype=jnp.int32)).astype(f32)
    cosine, sine = rope_tables(positions, HEAD_SIZE)
    cosine = jnp.concatenate([cosine, cosine], 1)
    sine = jnp.concatenate([-sine, sine], 1)
    segment_row = document_index[0]
    segment_pad = jnp.concatenate(
        [jnp.full((halo_count * shard_len,), -1, jnp.int32), segment_row], 0
    )
    key_seg = lax.dynamic_slice_in_dim(
        segment_pad, context_at * shard_len, (halo_count + 1) * shard_len, 0
    )
    query_seg = lax.dynamic_slice_in_dim(segment_row, context_at * shard_len, shard_len, 0)

    down_all = adapter_down_projections.reshape(3 * rank, width)
    adapted = jnp.einsum("ja,ma->jm", gathered, down_all, preferred_element_type=f32).astype(bf16)
    adapted_query = adapted[:, :rank]
    adapted_key = adapted[:, rank : 2 * rank]
    adapted_value = adapted[:, 2 * rank :]

    def projected(weight, low, up):
        return jnp.dot(gathered, weight, preferred_element_type=f32) + adapter_scale * jnp.dot(
            low, up, preferred_element_type=f32
        )

    key_linear = projected(key_value_weight[0], adapted_key, adapter_up_key_value[0])
    value_linear = projected(key_value_weight[1], adapted_value, adapter_up_key_value[1])
    pair_local = rope_pair(key_linear, value_linear, cosine, sine)
    earlier = [
        passed_along(pair_local, "context", distance) for distance in range(halo_count, 0, -1)
    ]
    queries = rope_query(
        projected(query_weight, adapted_query, adapter_up_query), cosine, sine
    )
    pairs = earlier + [pair_local]
    weights, attended = attention_forward(queries, pairs, query_seg[None, :], key_seg[:, None])
    factor = jnp.einsum(
        "kn,pn->kp", attended, adapter_down_output, preferred_element_type=f32
    ).astype(bf16)

    incoming, weights, attended, factor = lax.optimization_barrier(
        (incoming, weights, attended, factor)
    )
    up_gradient = (
        adapter_scale
        * jnp.einsum("ja,ma->jm", incoming, adapter_up_output, preferred_element_type=f32)
    ).astype(bf16)
    grad_attended = (
        jnp.einsum("td,hd->th", incoming, output_weight, preferred_element_type=f32)
        + jnp.dot(up_gradient, adapter_down_output, preferred_element_type=f32)
    ).astype(bf16)
    grad_query, grad_halo, grad_own = attention_backward(
        queries, grad_attended, attended, weights, pairs, cosine, sine
    )
    shares = [
        passed_along(
            lax.slice_in_dim(
                grad_halo,
                (halo_count - distance) * shard_len,
                (halo_count - distance + 1) * shard_len,
                axis=1,
            ),
            "context",
            -distance,
        )
        for distance in range(1, halo_count + 1)
    ]
    first_term = jnp.einsum("th,dh->td", grad_query, query_weight, preferred_element_type=f32)
    query_hidden = jnp.einsum(
        "kn,pn->kp", grad_query, adapter_up_query, preferred_element_type=f32
    )
    grad_key, grad_value = combine(grad_own, shares, cosine, sine)
    key_hidden = jnp.einsum(
        "kn,pn->kp", grad_key, adapter_up_key_value[0], preferred_element_type=f32
    )
    value_hidden = jnp.einsum(
        "kn,pn->kp", grad_value, adapter_up_key_value[1], preferred_element_type=f32
    )
    hidden = (
        adapter_scale * jnp.concatenate([query_hidden, key_hidden, value_hidden], 1)
    ).astype(bf16)
    term = term_sum(first_term, grad_key, grad_value, hidden, key_value_weight, down_all)
    grad_input = lax.psum_scatter(term, "tensor", scatter_dimension=0, tiled=True)[None]

    def over_tokens(low, grads):
        return jnp.einsum("tr,th->rh", low, grads, preferred_element_type=f32)

    wide = jnp.concatenate(
        [over_tokens(hidden, gathered), adapter_scale * over_tokens(factor, incoming)], 0
    ).astype(bf16)
    narrow = jnp.concatenate(
        [
            adapter_scale * over_tokens(adapted_query, grad_query),
            adapter_scale * over_tokens(adapted_key, grad_key),
            adapter_scale * over_tokens(adapted_value, grad_value),
            over_tokens(up_gradient, attended),
        ],
        1,
    ).astype(bf16)
    mine = scattered_rows(wide, "tensor").astype(bf16)
    size = mine.size
    flat = jnp.concatenate([mine.reshape(-1, 128), narrow.reshape(-1, 128)], 0)
    flat = summed_pairwise(summed_pairwise(flat, "context"), "dp")
    wide_sum = gathered_rows(flat[: size // 128].reshape(mine.shape), "tensor").astype(f32)
    narrow_sum = flat[size // 128 :].reshape(narrow.shape).astype(f32)
    q_cols, kv_cols = adapter_up_query.shape[1], adapter_up_key_value.shape[2]
    return (
        grad_input,
        wide_sum[: 3 * rank].reshape(3, rank, width),
        narrow_sum[:, :q_cols],
        jnp.stack(
            [
                narrow_sum[:, q_cols : q_cols + kv_cols],
                narrow_sum[:, q_cols + kv_cols : q_cols + 2 * kv_cols],
            ],
            0,
        ),
        narrow_sum[:, q_cols + 2 * kv_cols :],
        wide_sum[3 * rank :],
    )


def solution(mesh):
    in_specs = (
        P("dp", ("context", "tensor"), None),
        P("dp", ("context", "tensor"), None),
        P("dp", None),
        P(None, "tensor"),
        P(None, None, "tensor"),
        P("tensor", None),
        P(),
        P(None, "tensor"),
        P(None, None, "tensor"),
        P(None, "tensor"),
        P(),
    )
    out_specs = (
        P("dp", ("context", "tensor"), None),
        P(),
        P(None, "tensor"),
        P(None, None, "tensor"),
        P(None, "tensor"),
        P(),
    )
    return jax.shard_map(local, mesh=mesh, in_specs=in_specs, out_specs=out_specs, check_vma=False)
```

```python
import functools

import jax
import jax.numpy as jnp
from jax import lax
from jax.experimental import pallas as pl
from jax.experimental.pallas import tpu as pltpu
from jax.sharding import PartitionSpec as P

HEAD_SIZE = 128
WINDOW = 1024


adapter_scale = 2.0
attn_scale = 168.0 ** (-0.5)
rope_base = 10000.0


def passed_along(block, axis, distance):
    devices = range(lax.axis_size(axis))
    route = [(i - distance, i) for i in devices if i - distance in devices]
    return lax.ppermute(block, axis, route)


def rope_tables(positions, head_width):
    half_width = head_width // 2
    inverse = rope_base ** (-(jnp.arange(half_width, dtype=jnp.float32) * 2.0 / head_width))
    angle = positions[:, None] * inverse[None, :]
    return (jnp.cos(angle), jnp.sin(angle))


NT = (((1,), (1,)), ((), ()))
TN = (((0,), (0,)), ((), ()))
f32 = jnp.float32
bf16 = jnp.bfloat16


def dot(a, b, dims):
    return lax.dot_general(a, b, dims, preferred_element_type=f32)


def turned(x, cosine, sine):
    return x * cosine + pltpu.roll(x, x.shape[-1] // 2, 1) * sine


def rope_query_kernel(x_ref, cos_ref, sin_ref, out_ref):
    out_ref[...] = turned(x_ref[...], cos_ref[...], sin_ref[...]).astype(bf16)


def rope_pair_kernel(k_ref, v_ref, cos_ref, sin_ref, out_ref):
    out_ref[0] = turned(k_ref[...], cos_ref[...], sin_ref[...]).astype(bf16)
    out_ref[1] = v_ref[...].astype(bf16)


def rope_query(x, cosine, sine):
    rows, cols = x.shape
    table = pl.BlockSpec((rows, HEAD_SIZE), lambda h: (0, 0))
    return pl.pallas_call(
        rope_query_kernel,
        grid=(cols // HEAD_SIZE,),
        in_specs=[pl.BlockSpec((rows, HEAD_SIZE), lambda h: (0, h)), table, table],
        out_specs=pl.BlockSpec((rows, HEAD_SIZE), lambda h: (0, h)),
        out_shape=jax.ShapeDtypeStruct((rows, cols), bf16),
        name="rope_query",
        cost_estimate=pl.CostEstimate(flops=4 * rows * cols, bytes_accessed=6 * rows * cols, transcendentals=0),
    )(x, cosine, sine)


def rope_pair(k, v, cosine, sine):
    rows, cols = k.shape
    table = pl.BlockSpec((rows, HEAD_SIZE), lambda h: (0, 0))
    block = pl.BlockSpec((rows, HEAD_SIZE), lambda h: (0, h))
    return pl.pallas_call(
        rope_pair_kernel,
        grid=(cols // HEAD_SIZE,),
        in_specs=[block, block, table, table],
        out_specs=pl.BlockSpec((2, rows, HEAD_SIZE), lambda h: (0, 0, h)),
        out_shape=jax.ShapeDtypeStruct((2, rows, cols), bf16),
        name="rope_pair",
        cost_estimate=pl.CostEstimate(flops=4 * rows * cols, bytes_accessed=12 * rows * cols, transcendentals=0),
    )(k, v, cosine, sine)


def band(block, rows, halo_rows, keys):
    first = max(0, (halo_rows + block * rows - WINDOW + 1) // 128 * 128)
    return first, min(keys, halo_rows + (block + 1) * rows)


def fill(refs, k_buf, v_buf):
    at = 0
    for ref in refs:
        n = ref.shape[1]
        k_buf[at : at + n] = ref[0]
        v_buf[at : at + n] = ref[1]
        at += n


def forward_kernel(halo_rows, group, rows, *refs):
    q_ref, qseg_ref, kseg_ref = refs[:3]
    pair_refs = refs[3:-5]
    w_ref, att_ref, k_buf, v_buf, bias = refs[-5:]
    keys, count = bias.shape
    fill(pair_refs, k_buf, v_buf)

    @pl.when(pl.program_id(0) == 0)
    def _():
        for b in range(count // rows):
            lo, hi = band(b, rows, halo_rows, keys)
            shape = (hi - lo, rows)
            offset = (
                lax.broadcasted_iota(jnp.int32, shape, 1)
                - lax.broadcasted_iota(jnp.int32, shape, 0)
                + (halo_rows + b * rows - lo)
            )
            same = kseg_ref[lo:hi, :] == qseg_ref[:, b * rows : (b + 1) * rows]
            allowed = same & (offset >= 0) & (offset < WINDOW)
            bias[lo:hi, b * rows : (b + 1) * rows] = jnp.where(allowed, 0.0, -1e30)

    for g in range(group):
        for b in range(count // rows):
            lo, hi = band(b, rows, halo_rows, keys)
            here = slice(b * rows, (b + 1) * rows)
            cols = slice(g * HEAD_SIZE, (g + 1) * HEAD_SIZE)
            s = dot(k_buf[lo:hi], q_ref[here, cols], NT) * attn_scale + bias[lo:hi, here]
            p = jnp.exp(s - jnp.max(s, axis=0, keepdims=True))
            w = (p * (1.0 / jnp.sum(p, axis=0, keepdims=True))).astype(bf16)
            w_ref[g, lo:hi, here] = w
            att_ref[here, cols] = dot(v_buf[lo:hi], w, TN).T.astype(bf16)


def attention_forward(queries, pairs, query_seg, key_seg):
    count, q_cols = queries.shape
    kv_cols = pairs[0].shape[2]
    group = q_cols // kv_cols
    keys = count * len(pairs)
    rows = min(256, count)
    halo_rows = keys - count
    q_spec = pl.BlockSpec((count, group * HEAD_SIZE), lambda h: (0, h))
    pair_spec = pl.BlockSpec((2, count, HEAD_SIZE), lambda h: (0, 0, h))
    return pl.pallas_call(
        functools.partial(forward_kernel, halo_rows, group, rows),
        grid=(kv_cols // HEAD_SIZE,),
        in_specs=[
            q_spec,
            pl.BlockSpec((1, count), lambda h: (0, 0)),
            pl.BlockSpec((keys, 1), lambda h: (0, 0)),
        ]
        + [pair_spec] * len(pairs),
        out_specs=[pl.BlockSpec((group, keys, count), lambda h: (h, 0, 0)), q_spec],
        out_shape=[
            jax.ShapeDtypeStruct((q_cols // HEAD_SIZE, keys, count), bf16),
            jax.ShapeDtypeStruct((count, q_cols), bf16),
        ],
        scratch_shapes=[
            pltpu.VMEM((keys, HEAD_SIZE), bf16),
            pltpu.VMEM((keys, HEAD_SIZE), bf16),
            pltpu.VMEM((keys, count), f32),
        ],
        compiler_params=pltpu.CompilerParams(vmem_limit_bytes=48 << 20),
        name="attention_forward",
        cost_estimate=pl.CostEstimate(
            flops=4 * q_cols * count * keys, bytes_accessed=40 << 20, transcendentals=8 * count * keys
        ),
    )(queries, query_seg, key_seg, *pairs)


def backward_kernel(halo_rows, group, rows, n_pairs, *refs):
    q_ref, g_ref, att_ref, w_ref, cos_ref, sin_ref = refs[:6]
    pair_refs = refs[6 : 6 + n_pairs]
    dq_ref, halo_ref, own_ref, k_buf, v_buf, dk_buf, dv_buf = refs[6 + n_pairs :]
    keys = k_buf.shape[0]
    count = q_ref.shape[0]
    half = HEAD_SIZE // 2
    fill(pair_refs, k_buf, v_buf)
    dk_buf[...] = jnp.zeros_like(dk_buf)
    dv_buf[...] = jnp.zeros_like(dv_buf)
    for b in range(count // rows):
        lo, hi = band(b, rows, halo_rows, keys)
        here = slice(b * rows, (b + 1) * rows)
        for h in range(group):
            cols = slice(h * HEAD_SIZE, (h + 1) * HEAD_SIZE)
            g = g_ref[here, cols]
            w = w_ref[h, lo:hi, here]
            row_dot = jnp.sum((g.astype(f32) * att_ref[here, cols].astype(f32)).T, axis=0, keepdims=True)
            gw = dot(v_buf[lo:hi], g, NT)
            ds = (w.astype(f32) * ((gw - row_dot) * attn_scale)).astype(bf16)
            dv_buf[lo:hi] += dot(w, g, (((1,), (0,)), ((), ())))
            dk_buf[lo:hi] += dot(ds, q_ref[here, cols], (((1,), (0,)), ((), ())))
            dq = dot(k_buf[lo:hi], ds, TN).T
            dq_ref[here, cols] = turned(dq, cos_ref[here], -sin_ref[here]).astype(bf16)
    if halo_rows:
        halo_ref[0] = dk_buf[:halo_rows].astype(bf16)
        halo_ref[1] = dv_buf[:halo_rows].astype(bf16)
    own_ref[0] = dk_buf[halo_rows:]
    own_ref[1] = dv_buf[halo_rows:]


def attention_backward(queries, grads, attended, weights, pairs, cosine, sine, part, parts):
    count, q_cols = queries.shape
    kv_cols = pairs[0].shape[2]
    group = q_cols // kv_cols
    q_cols, kv_cols = q_cols // parts, kv_cols // parts
    heads = kv_cols // HEAD_SIZE
    first = part * heads
    keys = count * len(pairs)
    rows = min(256, count)
    halo_rows = keys - count
    q_in = pl.BlockSpec((count, group * HEAD_SIZE), lambda h: (0, h + first))
    q_out = pl.BlockSpec((count, group * HEAD_SIZE), lambda h: (0, h))
    pair_in = pl.BlockSpec((2, count, HEAD_SIZE), lambda h: (0, 0, h + first))
    pair_out = pl.BlockSpec((2, count, HEAD_SIZE), lambda h: (0, 0, h))
    table = pl.BlockSpec((count, HEAD_SIZE), lambda h: (0, 0))
    return pl.pallas_call(
        functools.partial(backward_kernel, halo_rows, group, rows, len(pairs)),
        grid=(heads,),
        in_specs=[
            q_in,
            q_in,
            q_in,
            pl.BlockSpec((group, keys, count), lambda h: (h + first, 0, 0)),
            table,
            table,
        ]
        + [pair_in] * len(pairs),
        out_specs=[
            q_out,
            pl.BlockSpec((2, halo_rows, HEAD_SIZE), lambda h: (0, 0, h)),
            pair_out,
        ],
        out_shape=[
            jax.ShapeDtypeStruct((count, q_cols), bf16),
            jax.ShapeDtypeStruct((2, halo_rows, kv_cols), bf16),
            jax.ShapeDtypeStruct((2, count, kv_cols), f32),
        ],
        scratch_shapes=[
            pltpu.VMEM((keys, HEAD_SIZE), bf16),
            pltpu.VMEM((keys, HEAD_SIZE), bf16),
            pltpu.VMEM((keys, HEAD_SIZE), f32),
            pltpu.VMEM((keys, HEAD_SIZE), f32),
        ],
        compiler_params=pltpu.CompilerParams(vmem_limit_bytes=48 << 20),
        name="attention_backward",
        cost_estimate=pl.CostEstimate(
            flops=8 * q_cols * count * keys, bytes_accessed=20 << 20, transcendentals=0
        ),
    )(queries, grads, attended, weights, cosine, sine, *pairs)


def combine_kernel(own_ref, cos_ref, sin_ref, *refs):
    dk_ref, dv_ref = refs[-2:]
    dk, dv = own_ref[0], own_ref[1]
    for ref in refs[:-2]:
        dk = dk + ref[0].astype(f32)
        dv = dv + ref[1].astype(f32)
    dk_ref[...] = turned(dk, cos_ref[...], -sin_ref[...]).astype(bf16)
    dv_ref[...] = dv.astype(bf16)


def combine(own, shares, cosine, sine):
    _, count, kv_cols = own.shape
    pair_spec = pl.BlockSpec((2, count, HEAD_SIZE), lambda h: (0, 0, h))
    table = pl.BlockSpec((count, HEAD_SIZE), lambda h: (0, 0))
    out = pl.BlockSpec((count, HEAD_SIZE), lambda h: (0, h))
    return pl.pallas_call(
        combine_kernel,
        grid=(kv_cols // HEAD_SIZE,),
        in_specs=[pair_spec, table, table] + [pair_spec] * len(shares),
        out_specs=[out, out],
        out_shape=[jax.ShapeDtypeStruct((count, kv_cols), bf16)] * 2,
        name="combine_pairs",
        cost_estimate=pl.CostEstimate(flops=8 * count * kv_cols, bytes_accessed=20 * count * kv_cols, transcendentals=0),
    )(own, cosine, sine, *shares)


def term_kernel(parts, *refs):
    first_ref, hid_ref, kv_ref, down_ref = refs[:4]
    out_ref = refs[-1]
    total = first_ref[...] + dot(hid_ref[...], down_ref[...], TN)
    cols = kv_ref.shape[2] // parts
    for p in range(parts):
        here = slice(p * cols, (p + 1) * cols)
        total = total + dot(refs[4 + p][...], kv_ref[0, :, here], NT)
        total = total + dot(refs[4 + parts + p][...], kv_ref[1, :, here], NT)
    out_ref[...] = total.astype(bf16)


def term_sum(first, dk, dv, hidden, kv_weight, down):
    count, width = first.shape
    tile = next(t for t in (896, 768, 384, 256, 128, width) if width % t == 0)
    whole = lambda a: pl.BlockSpec(a.shape, lambda i: (0, 0))
    return pl.pallas_call(
        functools.partial(term_kernel, len(dk)),
        grid=(width // tile,),
        in_specs=[
            pl.BlockSpec((count, tile), lambda i: (0, i)),
            whole(hidden),
            pl.BlockSpec((2, tile, kv_weight.shape[2]), lambda i: (0, i, 0)),
            pl.BlockSpec((down.shape[0], tile), lambda i: (0, i)),
        ]
        + [whole(a) for a in dk + dv],
        out_specs=pl.BlockSpec((count, tile), lambda i: (0, i)),
        out_shape=jax.ShapeDtypeStruct((count, width), bf16),
        compiler_params=pltpu.CompilerParams(vmem_limit_bytes=48 << 20),
        name="input_term",
        cost_estimate=pl.CostEstimate(
            flops=4 * count * width * kv_weight.shape[2],
            bytes_accessed=28 * width * count // 5,
            transcendentals=0,
        ),
    )(first, hidden, kv_weight, down, *dk, *dv)


def after(block, *others):
    anywhere = pl.BlockSpec(memory_space=pl.ANY)
    return pl.pallas_call(
        lambda *refs: None,
        in_specs=[anywhere] * (1 + len(others)),
        out_specs=anywhere,
        out_shape=jax.ShapeDtypeStruct(block.shape, block.dtype),
        input_output_aliases={0: 0},
        name="after",
        cost_estimate=pl.CostEstimate(flops=0, bytes_accessed=0, transcendentals=0),
    )(block, *others)


def summed_pairwise(block, axis):
    n = lax.axis_size(axis)
    if n & (n - 1):
        return lax.psum(block, axis)
    step = 1
    while step < n:
        other = lax.ppermute(block, axis, [(i, i ^ step) for i in range(n)])
        block = (block.astype(f32) + other.astype(f32)).astype(bf16)
        step *= 2
    return block


def scattered_rows(block, axis):
    n, me = lax.axis_size(axis), lax.axis_index(axis)
    if n & (n - 1):
        return lax.psum_scatter(block, axis, scatter_dimension=0, tiled=True)
    step = n // 2
    while step:
        halves = block.reshape(2, block.shape[0] // 2, block.shape[1])
        bit = (me // step) % 2
        keep = jnp.where(bit == 0, halves[0], halves[1])
        give = jnp.where(bit == 0, halves[1], halves[0])
        got = lax.ppermute(give, axis, [(i, i ^ step) for i in range(n)])
        block = (keep.astype(f32) + got.astype(f32)).astype(bf16)
        step //= 2
    return block


def gathered_rows(block, axis):
    n, me = lax.axis_size(axis), lax.axis_index(axis)
    if n & (n - 1):
        return lax.all_gather(block, axis, axis=0, tiled=True)
    step = 1
    while step < n:
        got = lax.ppermute(block, axis, [(i, i ^ step) for i in range(n)])
        first = (me // step) % 2 == 0
        block = jnp.concatenate([jnp.where(first, block, got), jnp.where(first, got, block)], 0)
        step *= 2
    return block


def local(
    tokens,
    output_gradient,
    document_index,
    query_weight,
    key_value_weight,
    output_weight,
    adapter_down_projections,
    adapter_up_query,
    adapter_up_key_value,
    adapter_down_output,
    adapter_up_output,
):
    tensor_size = lax.axis_size("tensor")
    context_at = lax.axis_index("context")
    local_count = tokens.shape[1]
    width = tokens.shape[2]
    shard_len = local_count * tensor_size
    halo_count = (WINDOW - 1) // shard_len + 1
    rank = adapter_down_projections.shape[1]
    gathered = lax.all_gather(tokens[0], "tensor", axis=0, tiled=True)
    incoming = lax.all_gather(output_gradient[0], "tensor", axis=0, tiled=True)
    positions = (context_at * shard_len + jnp.arange(shard_len, dtype=jnp.int32)).astype(f32)
    cosine, sine = rope_tables(positions, HEAD_SIZE)
    cosine = jnp.concatenate([cosine, cosine], 1)
    sine = jnp.concatenate([-sine, sine], 1)
    segment_row = document_index[0]
    segment_pad = jnp.concatenate(
        [jnp.full((halo_count * shard_len,), -1, jnp.int32), segment_row], 0
    )
    key_seg = lax.dynamic_slice_in_dim(
        segment_pad, context_at * shard_len, (halo_count + 1) * shard_len, 0
    )
    query_seg = lax.dynamic_slice_in_dim(segment_row, context_at * shard_len, shard_len, 0)

    down_all = adapter_down_projections.reshape(3 * rank, width)
    adapted = jnp.einsum("ja,ma->jm", gathered, down_all, preferred_element_type=f32).astype(bf16)
    adapted_query = adapted[:, :rank]
    adapted_key = adapted[:, rank : 2 * rank]
    adapted_value = adapted[:, 2 * rank :]

    def projected(weight, low, up):
        return jnp.dot(gathered, weight, preferred_element_type=f32) + adapter_scale * jnp.dot(
            low, up, preferred_element_type=f32
        )

    key_linear = projected(key_value_weight[0], adapted_key, adapter_up_key_value[0])
    value_linear = projected(key_value_weight[1], adapted_value, adapter_up_key_value[1])
    pair_local = rope_pair(key_linear, value_linear, cosine, sine)
    earlier = [
        passed_along(pair_local, "context", distance) for distance in range(halo_count, 0, -1)
    ]
    queries = rope_query(
        projected(query_weight, adapted_query, adapter_up_query), cosine, sine
    )
    pairs = earlier + [pair_local]
    weights, attended = attention_forward(queries, pairs, query_seg[None, :], key_seg[:, None])
    factor = jnp.einsum(
        "kn,pn->kp", attended, adapter_down_output, preferred_element_type=f32
    ).astype(bf16)

    incoming, weights, attended, factor = lax.optimization_barrier(
        (incoming, weights, attended, factor)
    )
    up_gradient = (
        adapter_scale
        * jnp.einsum("ja,ma->jm", incoming, adapter_up_output, preferred_element_type=f32)
    ).astype(bf16)
    grad_attended = (
        jnp.einsum("td,hd->th", incoming, output_weight, preferred_element_type=f32)
        + jnp.dot(up_gradient, adapter_down_output, preferred_element_type=f32)
    ).astype(bf16)
    kv_heads = key_value_weight.shape[2] // HEAD_SIZE
    parts = 2 if kv_heads % 2 == 0 else 1
    grad_queries, owns, arrivals = [], [], []
    for part in range(parts):
        grad_part, grad_halo, grad_own = attention_backward(
            queries, grad_attended, attended, weights, pairs, cosine, sine, part, parts
        )
        grad_queries.append(grad_part)
        owns.append(grad_own)
        arrivals.append(
            [
                passed_along(
                    lax.slice_in_dim(
                        grad_halo,
                        (halo_count - distance) * shard_len,
                        (halo_count - distance + 1) * shard_len,
                        axis=1,
                    ),
                    "context",
                    -distance,
                )
                for distance in range(1, halo_count + 1)
            ]
        )
    grad_query = jnp.concatenate(grad_queries, 1)
    first_term = jnp.einsum("th,dh->td", grad_query, query_weight, preferred_element_type=f32)
    grad_keys, grad_values = [], []
    for own, shares in zip(owns, arrivals):
        grad_key, grad_value = combine(own, shares, cosine, sine)
        grad_keys.append(grad_key)
        grad_values.append(grad_value)

    def lowered(up, grads):
        ups = jnp.split(up, len(grads), 1)
        return sum(
            jnp.einsum("pn,kn->pk", u, g, preferred_element_type=f32) for u, g in zip(ups, grads)
        )

    hidden = (
        adapter_scale
        * jnp.concatenate(
            [
                lowered(adapter_up_query, [grad_query]),
                lowered(adapter_up_key_value[0], grad_keys),
                lowered(adapter_up_key_value[1], grad_values),
            ],
            0,
        )
    ).astype(bf16)
    term = term_sum(first_term, grad_keys, grad_values, hidden, key_value_weight, down_all)
    grad_input = lax.psum_scatter(term, "tensor", scatter_dimension=0, tiled=True)[None]

    def over_tokens(low, grads):
        return jnp.einsum("tr,th->rh", low, grads, preferred_element_type=f32)

    low_rows = jnp.concatenate([hidden, (adapter_scale * factor.astype(f32)).astype(bf16).T], 0)
    low_rows = after(low_rows, term)
    mine_low = scattered_rows(low_rows, "tensor")
    row_at = lax.axis_index("tensor") * mine_low.shape[0] + jnp.arange(mine_low.shape[0])
    from_tokens = (row_at < 3 * rank)[:, None]
    zero = jnp.zeros_like(mine_low)
    mine = (
        jnp.dot(jnp.where(from_tokens, mine_low, zero), gathered, preferred_element_type=f32)
        + jnp.dot(jnp.where(from_tokens, zero, mine_low), incoming, preferred_element_type=f32)
    ).astype(bf16)
    narrow = jnp.concatenate(
        [adapter_scale * over_tokens(adapted_query, grad_query)]
        + [adapter_scale * over_tokens(adapted_key, g) for g in grad_keys]
        + [adapter_scale * over_tokens(adapted_value, g) for g in grad_values]
        + [over_tokens(up_gradient, attended)],
        1,
    ).astype(bf16)
    size = mine.size
    flat = jnp.concatenate([mine.reshape(-1, 128), narrow.reshape(-1, 128)], 0)
    flat = summed_pairwise(summed_pairwise(flat, "context"), "dp")
    wide_sum = gathered_rows(flat[: size // 128].reshape(mine.shape), "tensor").astype(f32)
    narrow_sum = flat[size // 128 :].reshape(narrow.shape).astype(f32)
    q_cols, kv_cols = adapter_up_query.shape[1], adapter_up_key_value.shape[2]
    return (
        grad_input,
        wide_sum[: 3 * rank].reshape(3, rank, width),
        narrow_sum[:, :q_cols],
        jnp.stack(
            [
                narrow_sum[:, q_cols : q_cols + kv_cols],
                narrow_sum[:, q_cols + kv_cols : q_cols + 2 * kv_cols],
            ],
            0,
        ),
        narrow_sum[:, q_cols + 2 * kv_cols :],
        wide_sum[3 * rank :],
    )


def solution(mesh):
    in_specs = (
        P("dp", ("context", "tensor"), None),
        P("dp", ("context", "tensor"), None),
        P("dp", None),
        P(None, "tensor"),
        P(None, None, "tensor"),
        P("tensor", None),
        P(),
        P(None, "tensor"),
        P(None, None, "tensor"),
        P(None, "tensor"),
        P(),
    )
    out_specs = (
        P("dp", ("context", "tensor"), None),
        P(),
        P(None, "tensor"),
        P(None, None, "tensor"),
        P(None, "tensor"),
        P(),
    )
    return jax.shard_map(local, mesh=mesh, in_specs=in_specs, out_specs=out_specs, check_vma=False)
```

```python
import functools

import jax
import jax.numpy as jnp
from jax import lax
from jax.experimental import pallas as pl
from jax.experimental.pallas import tpu as pltpu
from jax.sharding import PartitionSpec as P

HEAD_SIZE = 128
WINDOW = 1024


adapter_scale = 2.0
attn_scale = 168.0 ** (-0.5)
rope_base = 10000.0


def passed_along(block, axis, distance):
    devices = range(lax.axis_size(axis))
    route = [(i - distance, i) for i in devices if i - distance in devices]
    return lax.ppermute(block, axis, route)


def rope_tables(positions, head_width):
    half_width = head_width // 2
    inverse = rope_base ** (-(jnp.arange(half_width, dtype=jnp.float32) * 2.0 / head_width))
    angle = positions[:, None] * inverse[None, :]
    return (jnp.cos(angle), jnp.sin(angle))


NT = (((1,), (1,)), ((), ()))
TN = (((0,), (0,)), ((), ()))
f32 = jnp.float32
bf16 = jnp.bfloat16


def dot(a, b, dims):
    return lax.dot_general(a, b, dims, preferred_element_type=f32)


def turned(x, cosine, sine):
    return x * cosine + pltpu.roll(x, x.shape[-1] // 2, 1) * sine


def rope_query_kernel(x_ref, cos_ref, sin_ref, out_ref):
    out_ref[...] = turned(x_ref[...], cos_ref[...], sin_ref[...]).astype(bf16)


def rope_pair_kernel(k_ref, v_ref, cos_ref, sin_ref, out_ref):
    out_ref[0] = turned(k_ref[...], cos_ref[...], sin_ref[...]).astype(bf16)
    out_ref[1] = v_ref[...].astype(bf16)


def rope_query(x, cosine, sine):
    rows, cols = x.shape
    table = pl.BlockSpec((rows, HEAD_SIZE), lambda h: (0, 0))
    return pl.pallas_call(
        rope_query_kernel,
        grid=(cols // HEAD_SIZE,),
        in_specs=[pl.BlockSpec((rows, HEAD_SIZE), lambda h: (0, h)), table, table],
        out_specs=pl.BlockSpec((rows, HEAD_SIZE), lambda h: (0, h)),
        out_shape=jax.ShapeDtypeStruct((rows, cols), bf16),
        name="rope_query",
        cost_estimate=pl.CostEstimate(flops=4 * rows * cols, bytes_accessed=6 * rows * cols, transcendentals=0),
    )(x, cosine, sine)


def rope_pair(k, v, cosine, sine):
    rows, cols = k.shape
    table = pl.BlockSpec((rows, HEAD_SIZE), lambda h: (0, 0))
    block = pl.BlockSpec((rows, HEAD_SIZE), lambda h: (0, h))
    return pl.pallas_call(
        rope_pair_kernel,
        grid=(cols // HEAD_SIZE,),
        in_specs=[block, block, table, table],
        out_specs=pl.BlockSpec((2, rows, HEAD_SIZE), lambda h: (0, 0, h)),
        out_shape=jax.ShapeDtypeStruct((2, rows, cols), bf16),
        name="rope_pair",
        cost_estimate=pl.CostEstimate(flops=4 * rows * cols, bytes_accessed=12 * rows * cols, transcendentals=0),
    )(k, v, cosine, sine)


def band(block, rows, halo_rows, keys):
    first = max(0, (halo_rows + block * rows - WINDOW + 1) // 128 * 128)
    return first, min(keys, halo_rows + (block + 1) * rows)


def fill(refs, k_buf, v_buf):
    at = 0
    for ref in refs:
        n = ref.shape[1]
        k_buf[at : at + n] = ref[0]
        v_buf[at : at + n] = ref[1]
        at += n


def forward_kernel(halo_rows, group, rows, *refs):
    q_ref, qseg_ref, kseg_ref = refs[:3]
    pair_refs = refs[3:-5]
    w_ref, att_ref, k_buf, v_buf, bias = refs[-5:]
    keys, count = bias.shape
    fill(pair_refs, k_buf, v_buf)

    @pl.when(pl.program_id(0) == 0)
    def _():
        for b in range(count // rows):
            lo, hi = band(b, rows, halo_rows, keys)
            shape = (hi - lo, rows)
            offset = (
                lax.broadcasted_iota(jnp.int32, shape, 1)
                - lax.broadcasted_iota(jnp.int32, shape, 0)
                + (halo_rows + b * rows - lo)
            )
            same = kseg_ref[lo:hi, :] == qseg_ref[:, b * rows : (b + 1) * rows]
            allowed = same & (offset >= 0) & (offset < WINDOW)
            bias[lo:hi, b * rows : (b + 1) * rows] = jnp.where(allowed, 0.0, -1e30)

    for g in range(group):
        for b in range(count // rows):
            lo, hi = band(b, rows, halo_rows, keys)
            here = slice(b * rows, (b + 1) * rows)
            cols = slice(g * HEAD_SIZE, (g + 1) * HEAD_SIZE)
            s = dot(k_buf[lo:hi], q_ref[here, cols], NT) * attn_scale + bias[lo:hi, here]
            p = jnp.exp(s - jnp.max(s, axis=0, keepdims=True))
            w = (p * (1.0 / jnp.sum(p, axis=0, keepdims=True))).astype(bf16)
            w_ref[g, lo:hi, here] = w
            att_ref[here, cols] = dot(v_buf[lo:hi], w, TN).T.astype(bf16)


def attention_forward(queries, pairs, query_seg, key_seg):
    count, q_cols = queries.shape
    kv_cols = pairs[0].shape[2]
    group = q_cols // kv_cols
    keys = count * len(pairs)
    rows = min(256, count)
    halo_rows = keys - count
    q_spec = pl.BlockSpec((count, group * HEAD_SIZE), lambda h: (0, h))
    pair_spec = pl.BlockSpec((2, count, HEAD_SIZE), lambda h: (0, 0, h))
    return pl.pallas_call(
        functools.partial(forward_kernel, halo_rows, group, rows),
        grid=(kv_cols // HEAD_SIZE,),
        in_specs=[
            q_spec,
            pl.BlockSpec((1, count), lambda h: (0, 0)),
            pl.BlockSpec((keys, 1), lambda h: (0, 0)),
        ]
        + [pair_spec] * len(pairs),
        out_specs=[pl.BlockSpec((group, keys, count), lambda h: (h, 0, 0)), q_spec],
        out_shape=[
            jax.ShapeDtypeStruct((q_cols // HEAD_SIZE, keys, count), bf16),
            jax.ShapeDtypeStruct((count, q_cols), bf16),
        ],
        scratch_shapes=[
            pltpu.VMEM((keys, HEAD_SIZE), bf16),
            pltpu.VMEM((keys, HEAD_SIZE), bf16),
            pltpu.VMEM((keys, count), f32),
        ],
        compiler_params=pltpu.CompilerParams(vmem_limit_bytes=48 << 20),
        name="attention_forward",
        cost_estimate=pl.CostEstimate(
            flops=4 * q_cols * count * keys, bytes_accessed=40 << 20, transcendentals=8 * count * keys
        ),
    )(queries, query_seg, key_seg, *pairs)


def backward_kernel(halo_rows, group, rows, n_pairs, *refs):
    q_ref, g_ref, att_ref, w_ref, cos_ref, sin_ref = refs[:6]
    pair_refs = refs[6 : 6 + n_pairs]
    dq_ref, *halo_refs = refs[6 + n_pairs : 6 + 2 * n_pairs]
    own_ref, k_buf, v_buf, dk_buf, dv_buf = refs[6 + 2 * n_pairs :]
    keys = k_buf.shape[0]
    count = q_ref.shape[0]
    half = HEAD_SIZE // 2
    fill(pair_refs, k_buf, v_buf)
    dk_buf[...] = jnp.zeros_like(dk_buf)
    dv_buf[...] = jnp.zeros_like(dv_buf)
    for b in range(count // rows):
        lo, hi = band(b, rows, halo_rows, keys)
        here = slice(b * rows, (b + 1) * rows)
        for h in range(group):
            cols = slice(h * HEAD_SIZE, (h + 1) * HEAD_SIZE)
            g = g_ref[here, cols]
            w = w_ref[h, lo:hi, here]
            row_dot = jnp.sum((g.astype(f32) * att_ref[here, cols].astype(f32)).T, axis=0, keepdims=True)
            gw = dot(v_buf[lo:hi], g, NT)
            ds = (w.astype(f32) * ((gw - row_dot) * attn_scale)).astype(bf16)
            dv_buf[lo:hi] += dot(w, g, (((1,), (0,)), ((), ())))
            dk_buf[lo:hi] += dot(ds, q_ref[here, cols], (((1,), (0,)), ((), ())))
            dq = dot(k_buf[lo:hi], ds, TN).T
            dq_ref[here, cols] = turned(dq, cos_ref[here], -sin_ref[here]).astype(bf16)
    for at, halo_ref in enumerate(halo_refs):
        halo_ref[0] = dk_buf[at * count : (at + 1) * count].astype(bf16)
        halo_ref[1] = dv_buf[at * count : (at + 1) * count].astype(bf16)
    own_ref[0] = dk_buf[halo_rows:]
    own_ref[1] = dv_buf[halo_rows:]


def attention_backward(queries, grads, attended, weights, pairs, cosine, sine):
    count, q_cols = queries.shape
    kv_cols = pairs[0].shape[2]
    group = q_cols // kv_cols
    keys = count * len(pairs)
    rows = min(256, count)
    halo_rows = keys - count
    q_spec = pl.BlockSpec((count, group * HEAD_SIZE), lambda h: (0, h))
    pair_spec = pl.BlockSpec((2, count, HEAD_SIZE), lambda h: (0, 0, h))
    table = pl.BlockSpec((count, HEAD_SIZE), lambda h: (0, 0))
    return pl.pallas_call(
        functools.partial(backward_kernel, halo_rows, group, rows, len(pairs)),
        grid=(kv_cols // HEAD_SIZE,),
        in_specs=[
            q_spec,
            q_spec,
            q_spec,
            pl.BlockSpec((group, keys, count), lambda h: (h, 0, 0)),
            table,
            table,
        ]
        + [pair_spec] * len(pairs),
        out_specs=[q_spec] + [pair_spec] * len(pairs),
        out_shape=[jax.ShapeDtypeStruct((count, q_cols), bf16)]
        + [jax.ShapeDtypeStruct((2, count, kv_cols), bf16)] * (len(pairs) - 1)
        + [jax.ShapeDtypeStruct((2, count, kv_cols), f32)],
        scratch_shapes=[
            pltpu.VMEM((keys, HEAD_SIZE), bf16),
            pltpu.VMEM((keys, HEAD_SIZE), bf16),
            pltpu.VMEM((keys, HEAD_SIZE), f32),
            pltpu.VMEM((keys, HEAD_SIZE), f32),
        ],
        compiler_params=pltpu.CompilerParams(vmem_limit_bytes=48 << 20),
        name="attention_backward",
        cost_estimate=pl.CostEstimate(
            flops=8 * q_cols * count * keys, bytes_accessed=20 << 20, transcendentals=0
        ),
    )(queries, grads, attended, weights, cosine, sine, *pairs)


def term_kernel(*refs):
    first_ref, low_ref, kv_ref, down_ref, up_ref, cos_ref, sin_ref, own_ref = refs[:8]
    share_refs = refs[8:-4]
    out_ref, dk_ref, dv_ref, hid_ref = refs[-4:]
    rank = low_ref.shape[0]

    @pl.when(pl.program_id(0) == 0)
    def _():
        for h in range(dk_ref.shape[1] // HEAD_SIZE):
            cols = slice(h * HEAD_SIZE, (h + 1) * HEAD_SIZE)
            dk, dv = own_ref[0, :, cols], own_ref[1, :, cols]
            for ref in share_refs:
                dk = dk + ref[0, :, cols].astype(f32)
                dv = dv + ref[1, :, cols].astype(f32)
            dk_ref[:, cols] = turned(dk, cos_ref[...], -sin_ref[...]).astype(bf16)
            dv_ref[:, cols] = dv.astype(bf16)
        hid_ref[:rank] = low_ref[...].astype(bf16)
        hid_ref[rank : 2 * rank] = (adapter_scale * dot(up_ref[0], dk_ref[...], NT)).astype(bf16)
        hid_ref[2 * rank :] = (adapter_scale * dot(up_ref[1], dv_ref[...], NT)).astype(bf16)

    out_ref[...] = (
        dot(dk_ref[...], kv_ref[0], NT)
        + dot(dv_ref[...], kv_ref[1], NT)
        + dot(hid_ref[...], down_ref[...], TN)
        + first_ref[...].astype(f32)
    ).astype(bf16)


def term_sum(first, low, kv_weight, down, up, cosine, sine, own, shares):
    count, width = first.shape
    kv_cols = own.shape[2]
    rank = low.shape[0]
    tile = next(t for t in (768, 384, 256, 128, width) if width % t == 0)
    whole = lambda a: pl.BlockSpec(a.shape, lambda i: (0,) * len(a.shape))
    grad = jax.ShapeDtypeStruct((count, kv_cols), bf16)
    hidden = jax.ShapeDtypeStruct((3 * rank, count), bf16)
    return pl.pallas_call(
        term_kernel,
        grid=(width // tile,),
        in_specs=[
            pl.BlockSpec((count, tile), lambda i: (0, i)),
            whole(low),
            pl.BlockSpec((2, tile, kv_cols), lambda i: (0, i, 0)),
            pl.BlockSpec((down.shape[0], tile), lambda i: (0, i)),
            whole(up),
            whole(cosine),
            whole(sine),
            whole(own),
        ]
        + [whole(a) for a in shares],
        out_specs=[
            pl.BlockSpec((count, tile), lambda i: (0, i)),
            whole(grad),
            whole(grad),
            whole(hidden),
        ],
        out_shape=[jax.ShapeDtypeStruct((count, width), bf16), grad, grad, hidden],
        compiler_params=pltpu.CompilerParams(vmem_limit_bytes=48 << 20),
        name="input_term",
        cost_estimate=pl.CostEstimate(
            flops=4 * count * width * kv_cols, bytes_accessed=28 << 20, transcendentals=0
        ),
    )(first, low, kv_weight, down, up, cosine, sine, own, *shares)


def after(block, *others):
    anywhere = pl.BlockSpec(memory_space=pl.ANY)
    return pl.pallas_call(
        lambda *refs: None,
        in_specs=[anywhere] * (1 + len(others)),
        out_specs=anywhere,
        out_shape=jax.ShapeDtypeStruct(block.shape, block.dtype),
        input_output_aliases={0: 0},
        name="after",
        cost_estimate=pl.CostEstimate(flops=0, bytes_accessed=0, transcendentals=0),
    )(block, *others)


def summed_pairwise(block, axis):
    n = lax.axis_size(axis)
    if n & (n - 1):
        return lax.psum(block, axis)
    step = 1
    while step < n:
        other = lax.ppermute(block, axis, [(i, i ^ step) for i in range(n)])
        block = (block.astype(f32) + other.astype(f32)).astype(bf16)
        step *= 2
    return block


def scattered_rows(block, axis):
    n, me = lax.axis_size(axis), lax.axis_index(axis)
    if n & (n - 1):
        return lax.psum_scatter(block, axis, scatter_dimension=0, tiled=True)
    step = n // 2
    while step:
        halves = block.reshape(2, block.shape[0] // 2, block.shape[1])
        bit = (me // step) % 2
        keep = jnp.where(bit == 0, halves[0], halves[1])
        give = jnp.where(bit == 0, halves[1], halves[0])
        got = lax.ppermute(give, axis, [(i, i ^ step) for i in range(n)])
        block = (keep.astype(f32) + got.astype(f32)).astype(bf16)
        step //= 2
    return block


def gathered_rows(block, axis):
    n, me = lax.axis_size(axis), lax.axis_index(axis)
    if n & (n - 1):
        return lax.all_gather(block, axis, axis=0, tiled=True)
    step = 1
    while step < n:
        got = lax.ppermute(block, axis, [(i, i ^ step) for i in range(n)])
        first = (me // step) % 2 == 0
        block = jnp.concatenate([jnp.where(first, block, got), jnp.where(first, got, block)], 0)
        step *= 2
    return block


def local(
    tokens,
    output_gradient,
    document_index,
    query_weight,
    key_value_weight,
    output_weight,
    adapter_down_projections,
    adapter_up_query,
    adapter_up_key_value,
    adapter_down_output,
    adapter_up_output,
):
    tensor_size = lax.axis_size("tensor")
    context_at = lax.axis_index("context")
    local_count = tokens.shape[1]
    width = tokens.shape[2]
    shard_len = local_count * tensor_size
    halo_count = (WINDOW - 1) // shard_len + 1
    rank = adapter_down_projections.shape[1]
    gathered = lax.all_gather(tokens[0], "tensor", axis=0, tiled=True)
    incoming = lax.all_gather(output_gradient[0], "tensor", axis=0, tiled=True)
    positions = (context_at * shard_len + jnp.arange(shard_len, dtype=jnp.int32)).astype(f32)
    cosine, sine = rope_tables(positions, HEAD_SIZE)
    cosine = jnp.concatenate([cosine, cosine], 1)
    sine = jnp.concatenate([-sine, sine], 1)
    segment_row = document_index[0]
    segment_pad = jnp.concatenate(
        [jnp.full((halo_count * shard_len,), -1, jnp.int32), segment_row], 0
    )
    key_seg = lax.dynamic_slice_in_dim(
        segment_pad, context_at * shard_len, (halo_count + 1) * shard_len, 0
    )
    query_seg = lax.dynamic_slice_in_dim(segment_row, context_at * shard_len, shard_len, 0)

    down_all = adapter_down_projections.reshape(3 * rank, width)
    adapted = jnp.einsum("ja,ma->jm", gathered, down_all, preferred_element_type=f32).astype(bf16)
    adapted_query = adapted[:, :rank]
    adapted_key = adapted[:, rank : 2 * rank]
    adapted_value = adapted[:, 2 * rank :]

    def projected(weight, low, up):
        return jnp.dot(gathered, weight, preferred_element_type=f32) + adapter_scale * jnp.dot(
            low, up, preferred_element_type=f32
        )

    key_linear = projected(key_value_weight[0], adapted_key, adapter_up_key_value[0])
    value_linear = projected(key_value_weight[1], adapted_value, adapter_up_key_value[1])
    pair_local = rope_pair(key_linear, value_linear, cosine, sine)
    earlier = [
        passed_along(pair_local, "context", distance) for distance in range(halo_count, 0, -1)
    ]
    queries = rope_query(
        projected(query_weight, adapted_query, adapter_up_query), cosine, sine
    )
    pairs = earlier + [pair_local]
    weights, attended = attention_forward(queries, pairs, query_seg[None, :], key_seg[:, None])
    factor = jnp.einsum(
        "kn,pn->kp", attended, adapter_down_output, preferred_element_type=f32
    ).astype(bf16)

    incoming, weights, attended, factor = lax.optimization_barrier(
        (incoming, weights, attended, factor)
    )
    up_gradient = (
        adapter_scale
        * jnp.einsum("ja,ma->jm", incoming, adapter_up_output, preferred_element_type=f32)
    ).astype(bf16)
    grad_attended = (
        jnp.einsum("td,hd->th", incoming, output_weight, preferred_element_type=f32)
        + jnp.dot(up_gradient, adapter_down_output, preferred_element_type=f32)
    ).astype(bf16)
    grad_query, *grad_halos, grad_own = attention_backward(
        queries, grad_attended, attended, weights, pairs, cosine, sine
    )
    shares = [
        passed_along(grad_halos[halo_count - distance], "context", -distance)
        for distance in range(1, halo_count + 1)
    ]
    first_term = jnp.einsum(
        "th,dh->td", grad_query, query_weight, preferred_element_type=f32
    ).astype(bf16)
    query_low = adapter_scale * jnp.einsum(
        "pn,kn->pk", adapter_up_query, grad_query, preferred_element_type=f32
    )
    term, grad_key, grad_value, hidden = term_sum(
        first_term,
        query_low,
        key_value_weight,
        down_all,
        adapter_up_key_value,
        cosine,
        sine,
        grad_own,
        shares,
    )
    grad_input = lax.psum_scatter(term, "tensor", scatter_dimension=0, tiled=True)[None]

    def over_tokens(low, grads):
        return jnp.einsum("tr,th->rh", low, grads, preferred_element_type=f32)

    low_rows = jnp.concatenate([hidden, (adapter_scale * factor.astype(f32)).astype(bf16).T], 0)
    low_rows = after(low_rows, term)
    mine_low = scattered_rows(low_rows, "tensor")
    row_at = lax.axis_index("tensor") * mine_low.shape[0] + jnp.arange(mine_low.shape[0])
    from_tokens = (row_at < 3 * rank)[:, None]
    zero = jnp.zeros_like(mine_low)
    mine = (
        jnp.dot(jnp.where(from_tokens, mine_low, zero), gathered, preferred_element_type=f32)
        + jnp.dot(jnp.where(from_tokens, zero, mine_low), incoming, preferred_element_type=f32)
    ).astype(bf16)
    narrow = jnp.concatenate(
        [adapter_scale * over_tokens(adapted_query, grad_query)]
        + [adapter_scale * over_tokens(adapted_key, grad_key)]
        + [adapter_scale * over_tokens(adapted_value, grad_value)]
        + [over_tokens(up_gradient, attended)],
        1,
    ).astype(bf16)
    size = mine.size
    flat = jnp.concatenate([mine.reshape(-1, 128), narrow.reshape(-1, 128)], 0)
    flat = summed_pairwise(summed_pairwise(flat, "context"), "dp")
    wide_sum = gathered_rows(flat[: size // 128].reshape(mine.shape), "tensor").astype(f32)
    narrow_sum = flat[size // 128 :].reshape(narrow.shape).astype(f32)
    q_cols, kv_cols = adapter_up_query.shape[1], adapter_up_key_value.shape[2]
    return (
        grad_input,
        wide_sum[: 3 * rank].reshape(3, rank, width),
        narrow_sum[:, :q_cols],
        jnp.stack(
            [
                narrow_sum[:, q_cols : q_cols + kv_cols],
                narrow_sum[:, q_cols + kv_cols : q_cols + 2 * kv_cols],
            ],
            0,
        ),
        narrow_sum[:, q_cols + 2 * kv_cols :],
        wide_sum[3 * rank :],
    )


def solution(mesh):
    in_specs = (
        P("dp", ("context", "tensor"), None),
        P("dp", ("context", "tensor"), None),
        P("dp", None),
        P(None, "tensor"),
        P(None, None, "tensor"),
        P("tensor", None),
        P(),
        P(None, "tensor"),
        P(None, None, "tensor"),
        P(None, "tensor"),
        P(),
    )
    out_specs = (
        P("dp", ("context", "tensor"), None),
        P(),
        P(None, "tensor"),
        P(None, None, "tensor"),
        P(None, "tensor"),
        P(),
    )
    return jax.shard_map(local, mesh=mesh, in_specs=in_specs, out_specs=out_specs, check_vma=False)
```

```python
import functools

import jax
import jax.numpy as jnp
from jax import lax
from jax.experimental import pallas as pl
from jax.experimental.pallas import tpu as pltpu
from jax.sharding import PartitionSpec as P

HEAD_SIZE = 128
WINDOW = 1024


adapter_scale = 2.0
attn_scale = 168.0 ** (-0.5)
rope_base = 10000.0


def passed_along(block, axis, distance):
    devices = range(lax.axis_size(axis))
    route = [(i - distance, i) for i in devices if i - distance in devices]
    return lax.ppermute(block, axis, route)


def rope_tables(positions, head_width):
    half_width = head_width // 2
    inverse = rope_base ** (-(jnp.arange(half_width, dtype=jnp.float32) * 2.0 / head_width))
    angle = positions[:, None] * inverse[None, :]
    return (jnp.cos(angle), jnp.sin(angle))


NT = (((1,), (1,)), ((), ()))
TN = (((0,), (0,)), ((), ()))
f32 = jnp.float32
bf16 = jnp.bfloat16


def dot(a, b, dims):
    return lax.dot_general(a, b, dims, preferred_element_type=f32)


def turned(x, cosine, sine):
    return x * cosine + pltpu.roll(x, x.shape[-1] // 2, 1) * sine


def rope_query_kernel(x_ref, cos_ref, sin_ref, out_ref):
    out_ref[...] = turned(x_ref[...], cos_ref[...], sin_ref[...]).astype(bf16)


def rope_pair_kernel(k_ref, v_ref, cos_ref, sin_ref, out_ref):
    out_ref[0] = turned(k_ref[...], cos_ref[...], sin_ref[...]).astype(bf16)
    out_ref[1] = v_ref[...].astype(bf16)


def rope_query(x, cosine, sine):
    rows, cols = x.shape
    table = pl.BlockSpec((rows, HEAD_SIZE), lambda h: (0, 0))
    return pl.pallas_call(
        rope_query_kernel,
        grid=(cols // HEAD_SIZE,),
        in_specs=[pl.BlockSpec((rows, HEAD_SIZE), lambda h: (0, h)), table, table],
        out_specs=pl.BlockSpec((rows, HEAD_SIZE), lambda h: (0, h)),
        out_shape=jax.ShapeDtypeStruct((rows, cols), bf16),
        name="rope_query",
        cost_estimate=pl.CostEstimate(flops=4 * rows * cols, bytes_accessed=6 * rows * cols, transcendentals=0),
    )(x, cosine, sine)


def rope_pair(k, v, cosine, sine):
    rows, cols = k.shape
    table = pl.BlockSpec((rows, HEAD_SIZE), lambda h: (0, 0))
    block = pl.BlockSpec((rows, HEAD_SIZE), lambda h: (0, h))
    return pl.pallas_call(
        rope_pair_kernel,
        grid=(cols // HEAD_SIZE,),
        in_specs=[block, block, table, table],
        out_specs=pl.BlockSpec((2, rows, HEAD_SIZE), lambda h: (0, 0, h)),
        out_shape=jax.ShapeDtypeStruct((2, rows, cols), bf16),
        name="rope_pair",
        cost_estimate=pl.CostEstimate(flops=4 * rows * cols, bytes_accessed=12 * rows * cols, transcendentals=0),
    )(k, v, cosine, sine)


def band(block, rows, halo_rows, keys):
    first = max(0, (halo_rows + block * rows - WINDOW + 1) // 128 * 128)
    return first, min(keys, halo_rows + (block + 1) * rows)


def fill(refs, k_buf, v_buf):
    at = 0
    for ref in refs:
        n = ref.shape[1]
        k_buf[at : at + n] = ref[0]
        v_buf[at : at + n] = ref[1]
        at += n


def forward_kernel(halo_rows, group, rows, *refs):
    q_ref, qseg_ref, kseg_ref = refs[:3]
    pair_refs = refs[3:-5]
    w_ref, att_ref, k_buf, v_buf, bias = refs[-5:]
    keys, count = bias.shape
    fill(pair_refs, k_buf, v_buf)

    @pl.when(pl.program_id(0) == 0)
    def _():
        for b in range(count // rows):
            lo, hi = band(b, rows, halo_rows, keys)
            shape = (hi - lo, rows)
            offset = (
                lax.broadcasted_iota(jnp.int32, shape, 1)
                - lax.broadcasted_iota(jnp.int32, shape, 0)
                + (halo_rows + b * rows - lo)
            )
            same = kseg_ref[lo:hi, :] == qseg_ref[:, b * rows : (b + 1) * rows]
            allowed = same & (offset >= 0) & (offset < WINDOW)
            bias[lo:hi, b * rows : (b + 1) * rows] = jnp.where(allowed, 0.0, -1e30)

    for g in range(group):
        for b in range(count // rows):
            lo, hi = band(b, rows, halo_rows, keys)
            here = slice(b * rows, (b + 1) * rows)
            cols = slice(g * HEAD_SIZE, (g + 1) * HEAD_SIZE)
            s = dot(k_buf[lo:hi], q_ref[here, cols], NT) * attn_scale + bias[lo:hi, here]
            p = jnp.exp(s - jnp.max(s, axis=0, keepdims=True))
            w = (p * (1.0 / jnp.sum(p, axis=0, keepdims=True))).astype(bf16)
            w_ref[g, lo:hi, here] = w
            att_ref[here, cols] = dot(v_buf[lo:hi], w, TN).T.astype(bf16)


def attention_forward(queries, pairs, query_seg, key_seg):
    count, q_cols = queries.shape
    kv_cols = pairs[0].shape[2]
    group = q_cols // kv_cols
    keys = count * len(pairs)
    rows = min(256, count)
    halo_rows = keys - count
    q_spec = pl.BlockSpec((count, group * HEAD_SIZE), lambda h: (0, h))
    pair_spec = pl.BlockSpec((2, count, HEAD_SIZE), lambda h: (0, 0, h))
    return pl.pallas_call(
        functools.partial(forward_kernel, halo_rows, group, rows),
        grid=(kv_cols // HEAD_SIZE,),
        in_specs=[
            q_spec,
            pl.BlockSpec((1, count), lambda h: (0, 0)),
            pl.BlockSpec((keys, 1), lambda h: (0, 0)),
        ]
        + [pair_spec] * len(pairs),
        out_specs=[pl.BlockSpec((group, keys, count), lambda h: (h, 0, 0)), q_spec],
        out_shape=[
            jax.ShapeDtypeStruct((q_cols // HEAD_SIZE, keys, count), bf16),
            jax.ShapeDtypeStruct((count, q_cols), bf16),
        ],
        scratch_shapes=[
            pltpu.VMEM((keys, HEAD_SIZE), bf16),
            pltpu.VMEM((keys, HEAD_SIZE), bf16),
            pltpu.VMEM((keys, count), f32),
        ],
        compiler_params=pltpu.CompilerParams(vmem_limit_bytes=48 << 20),
        name="attention_forward",
        cost_estimate=pl.CostEstimate(
            flops=4 * q_cols * count * keys, bytes_accessed=40 << 20, transcendentals=8 * count * keys
        ),
    )(queries, query_seg, key_seg, *pairs)


def backward_kernel(halo_rows, group, rows, n_pairs, *refs):
    q_ref, g_ref, att_ref, w_ref, cos_ref, sin_ref = refs[:6]
    pair_refs = refs[6 : 6 + n_pairs]
    dq_ref, *halo_refs = refs[6 + n_pairs : 6 + 2 * n_pairs]
    own_ref, k_buf, v_buf, dk_buf, dv_buf = refs[6 + 2 * n_pairs :]
    keys = k_buf.shape[0]
    count = q_ref.shape[0]
    half = HEAD_SIZE // 2
    fill(pair_refs, k_buf, v_buf)
    dk_buf[...] = jnp.zeros_like(dk_buf)
    dv_buf[...] = jnp.zeros_like(dv_buf)
    for b in range(count // rows):
        lo, hi = band(b, rows, halo_rows, keys)
        here = slice(b * rows, (b + 1) * rows)
        for h in range(group):
            cols = slice(h * HEAD_SIZE, (h + 1) * HEAD_SIZE)
            g = g_ref[here, cols]
            w = w_ref[h, lo:hi, here]
            row_dot = jnp.sum((g.astype(f32) * att_ref[here, cols].astype(f32)).T, axis=0, keepdims=True)
            gw = dot(v_buf[lo:hi], g, NT)
            ds = (w.astype(f32) * ((gw - row_dot) * attn_scale)).astype(bf16)
            dv_buf[lo:hi] += dot(w, g, (((1,), (0,)), ((), ())))
            dk_buf[lo:hi] += dot(ds, q_ref[here, cols], (((1,), (0,)), ((), ())))
            dq = dot(k_buf[lo:hi], ds, TN).T
            dq_ref[here, cols] = turned(dq, cos_ref[here], -sin_ref[here]).astype(bf16)
    for at, halo_ref in enumerate(halo_refs):
        halo_ref[0] = dk_buf[at * count : (at + 1) * count].astype(bf16)
        halo_ref[1] = dv_buf[at * count : (at + 1) * count].astype(bf16)
    own_ref[0] = dk_buf[halo_rows:]
    own_ref[1] = dv_buf[halo_rows:]


def attention_backward(queries, grads, attended, weights, pairs, cosine, sine):
    count, q_cols = queries.shape
    kv_cols = pairs[0].shape[2]
    group = q_cols // kv_cols
    keys = count * len(pairs)
    rows = min(256, count)
    halo_rows = keys - count
    q_spec = pl.BlockSpec((count, group * HEAD_SIZE), lambda h: (0, h))
    pair_spec = pl.BlockSpec((2, count, HEAD_SIZE), lambda h: (0, 0, h))
    table = pl.BlockSpec((count, HEAD_SIZE), lambda h: (0, 0))
    return pl.pallas_call(
        functools.partial(backward_kernel, halo_rows, group, rows, len(pairs)),
        grid=(kv_cols // HEAD_SIZE,),
        in_specs=[
            q_spec,
            q_spec,
            q_spec,
            pl.BlockSpec((group, keys, count), lambda h: (h, 0, 0)),
            table,
            table,
        ]
        + [pair_spec] * len(pairs),
        out_specs=[q_spec] + [pair_spec] * len(pairs),
        out_shape=[jax.ShapeDtypeStruct((count, q_cols), bf16)]
        + [jax.ShapeDtypeStruct((2, count, kv_cols), bf16)] * (len(pairs) - 1)
        + [jax.ShapeDtypeStruct((2, count, kv_cols), f32)],
        scratch_shapes=[
            pltpu.VMEM((keys, HEAD_SIZE), bf16),
            pltpu.VMEM((keys, HEAD_SIZE), bf16),
            pltpu.VMEM((keys, HEAD_SIZE), f32),
            pltpu.VMEM((keys, HEAD_SIZE), f32),
        ],
        compiler_params=pltpu.CompilerParams(vmem_limit_bytes=48 << 20),
        name="attention_backward",
        cost_estimate=pl.CostEstimate(
            flops=8 * q_cols * count * keys, bytes_accessed=20 << 20, transcendentals=0
        ),
    )(queries, grads, attended, weights, cosine, sine, *pairs)


def term_kernel(*refs):
    first_ref, low_ref, kv_ref, down_ref, up_ref, cos_ref, sin_ref, own_ref = refs[:8]
    share_refs = refs[8:-4]
    out_ref, dk_ref, dv_ref, hid_ref = refs[-4:]
    rank = low_ref.shape[0]

    @pl.when(pl.program_id(0) == 0)
    def _():
        for h in range(dk_ref.shape[1] // HEAD_SIZE):
            cols = slice(h * HEAD_SIZE, (h + 1) * HEAD_SIZE)
            dk, dv = own_ref[0, :, cols], own_ref[1, :, cols]
            for ref in share_refs:
                dk = dk + ref[0, :, cols].astype(f32)
                dv = dv + ref[1, :, cols].astype(f32)
            dk_ref[:, cols] = turned(dk, cos_ref[...], -sin_ref[...]).astype(bf16)
            dv_ref[:, cols] = dv.astype(bf16)
        hid_ref[:rank] = low_ref[...].astype(bf16)
        hid_ref[rank : 2 * rank] = (adapter_scale * dot(up_ref[0], dk_ref[...], NT)).astype(bf16)
        hid_ref[2 * rank :] = (adapter_scale * dot(up_ref[1], dv_ref[...], NT)).astype(bf16)

    out_ref[...] = (
        dot(dk_ref[...], kv_ref[0], NT)
        + dot(dv_ref[...], kv_ref[1], NT)
        + dot(hid_ref[...], down_ref[...], TN)
        + first_ref[...].astype(f32)
    ).astype(bf16)


def term_sum(first, low, kv_weight, down, up, cosine, sine, own, shares):
    count, width = first.shape
    kv_cols = own.shape[2]
    rank = low.shape[0]
    tile = next(t for t in (768, 384, 256, 128, width) if width % t == 0)
    whole = lambda a: pl.BlockSpec(a.shape, lambda i: (0,) * len(a.shape))
    grad = jax.ShapeDtypeStruct((count, kv_cols), bf16)
    hidden = jax.ShapeDtypeStruct((3 * rank, count), bf16)
    return pl.pallas_call(
        term_kernel,
        grid=(width // tile,),
        in_specs=[
            pl.BlockSpec((count, tile), lambda i: (0, i)),
            whole(low),
            pl.BlockSpec((2, tile, kv_cols), lambda i: (0, i, 0)),
            pl.BlockSpec((down.shape[0], tile), lambda i: (0, i)),
            whole(up),
            whole(cosine),
            whole(sine),
            whole(own),
        ]
        + [whole(a) for a in shares],
        out_specs=[
            pl.BlockSpec((count, tile), lambda i: (0, i)),
            whole(grad),
            whole(grad),
            whole(hidden),
        ],
        out_shape=[jax.ShapeDtypeStruct((count, width), bf16), grad, grad, hidden],
        compiler_params=pltpu.CompilerParams(vmem_limit_bytes=48 << 20),
        name="input_term",
        cost_estimate=pl.CostEstimate(
            flops=4 * count * width * kv_cols, bytes_accessed=28 << 20, transcendentals=0
        ),
    )(first, low, kv_weight, down, up, cosine, sine, own, *shares)


def after(block, *others):
    anywhere = pl.BlockSpec(memory_space=pl.ANY)
    return pl.pallas_call(
        lambda *refs: None,
        in_specs=[anywhere] * (1 + len(others)),
        out_specs=anywhere,
        out_shape=jax.ShapeDtypeStruct(block.shape, block.dtype),
        input_output_aliases={0: 0},
        name="after",
        cost_estimate=pl.CostEstimate(flops=0, bytes_accessed=0, transcendentals=0),
    )(block, *others)


def summed_pairwise(block, axis):
    n = lax.axis_size(axis)
    if n & (n - 1):
        return lax.psum(block, axis)
    step = 1
    while step < n:
        other = lax.ppermute(block, axis, [(i, i ^ step) for i in range(n)])
        block = (block.astype(f32) + other.astype(f32)).astype(bf16)
        step *= 2
    return block


def scattered_rows(block, axis):
    n, me = lax.axis_size(axis), lax.axis_index(axis)
    if n & (n - 1):
        return lax.psum_scatter(block, axis, scatter_dimension=0, tiled=True)
    step = n // 2
    while step:
        halves = block.reshape(2, block.shape[0] // 2, block.shape[1])
        bit = (me // step) % 2
        keep = jnp.where(bit == 0, halves[0], halves[1])
        give = jnp.where(bit == 0, halves[1], halves[0])
        got = lax.ppermute(give, axis, [(i, i ^ step) for i in range(n)])
        block = (keep.astype(f32) + got.astype(f32)).astype(bf16)
        step //= 2
    return block


def gathered_rows(block, axis):
    n, me = lax.axis_size(axis), lax.axis_index(axis)
    lower, higher = [], []
    up = down = block
    for t in range(1, n):
        up = lax.ppermute(up, axis, [(i, i + 1) for i in range(t - 1, n - 1)])
        down = lax.ppermute(down, axis, [(i, i - 1) for i in range(1, n - t + 1)])
        lower.append(up)
        higher.append(down)
    rows = block.shape[0]
    line = jnp.concatenate(lower[::-1] + [block] + higher, 0)
    return lax.dynamic_slice_in_dim(line, (n - 1 - me) * rows, n * rows, 0)


def returned_shares(halos):
    n = lax.axis_size("context")
    if len(halos) != 2:
        count = len(halos)
        sent = [halos[count - d] for d in range(1, count + 1)]
        return [passed_along(b, "context", -d) for d, b in enumerate(sent, 1)], sent[0]
    far, near = halos
    relayed = lax.ppermute(far, "context", [(i, i - 1) for i in range(3, n, 2)])
    direct = lax.ppermute(far, "context", [(i, i - 2) for i in range(2, n, 2)])
    near = (near.astype(f32) + relayed.astype(f32)).astype(bf16)
    return [lax.ppermute(near, "context", [(i, i - 1) for i in range(1, n)]), direct], near


def local(
    tokens,
    output_gradient,
    document_index,
    query_weight,
    key_value_weight,
    output_weight,
    adapter_down_projections,
    adapter_up_query,
    adapter_up_key_value,
    adapter_down_output,
    adapter_up_output,
):
    tensor_size = lax.axis_size("tensor")
    context_at = lax.axis_index("context")
    local_count = tokens.shape[1]
    width = tokens.shape[2]
    shard_len = local_count * tensor_size
    halo_count = (WINDOW - 1) // shard_len + 1
    rank = adapter_down_projections.shape[1]
    gathered = lax.all_gather(tokens[0], "tensor", axis=0, tiled=True)
    incoming = lax.all_gather(output_gradient[0], "tensor", axis=0, tiled=True)
    positions = (context_at * shard_len + jnp.arange(shard_len, dtype=jnp.int32)).astype(f32)
    cosine, sine = rope_tables(positions, HEAD_SIZE)
    cosine = jnp.concatenate([cosine, cosine], 1)
    sine = jnp.concatenate([-sine, sine], 1)
    segment_row = document_index[0]
    segment_pad = jnp.concatenate(
        [jnp.full((halo_count * shard_len,), -1, jnp.int32), segment_row], 0
    )
    key_seg = lax.dynamic_slice_in_dim(
        segment_pad, context_at * shard_len, (halo_count + 1) * shard_len, 0
    )
    query_seg = lax.dynamic_slice_in_dim(segment_row, context_at * shard_len, shard_len, 0)

    down_all = adapter_down_projections.reshape(3 * rank, width)
    adapted = jnp.einsum("ja,ma->jm", gathered, down_all, preferred_element_type=f32).astype(bf16)
    adapted_query = adapted[:, :rank]
    adapted_key = adapted[:, rank : 2 * rank]
    adapted_value = adapted[:, 2 * rank :]

    def projected(weight, low, up):
        return jnp.dot(gathered, weight, preferred_element_type=f32) + adapter_scale * jnp.dot(
            low, up, preferred_element_type=f32
        )

    key_linear = projected(key_value_weight[0], adapted_key, adapter_up_key_value[0])
    value_linear = projected(key_value_weight[1], adapted_value, adapter_up_key_value[1])
    pair_local = rope_pair(key_linear, value_linear, cosine, sine)
    earlier = [
        passed_along(pair_local, "context", distance) for distance in range(halo_count, 0, -1)
    ]
    queries = rope_query(
        projected(query_weight, adapted_query, adapter_up_query), cosine, sine
    )
    pairs = earlier + [pair_local]
    weights, attended = attention_forward(queries, pairs, query_seg[None, :], key_seg[:, None])
    factor = jnp.einsum(
        "kn,pn->kp", attended, adapter_down_output, preferred_element_type=f32
    ).astype(bf16)

    incoming, weights, attended, factor = lax.optimization_barrier(
        (incoming, weights, attended, factor)
    )
    up_gradient = (
        adapter_scale
        * jnp.einsum("ja,ma->jm", incoming, adapter_up_output, preferred_element_type=f32)
    ).astype(bf16)
    grad_attended = (
        jnp.einsum("td,hd->th", incoming, output_weight, preferred_element_type=f32)
        + jnp.dot(up_gradient, adapter_down_output, preferred_element_type=f32)
    ).astype(bf16)
    grad_query, *grad_halos, grad_own = attention_backward(
        queries, grad_attended, attended, weights, pairs, cosine, sine
    )
    shares, last_sent = returned_shares(grad_halos)
    grad_query = after(grad_query, last_sent)
    first_term = jnp.einsum(
        "th,dh->td", grad_query, query_weight, preferred_element_type=f32
    ).astype(bf16)
    query_low = adapter_scale * jnp.einsum(
        "pn,kn->pk", adapter_up_query, grad_query, preferred_element_type=f32
    )
    term, grad_key, grad_value, hidden = term_sum(
        first_term,
        query_low,
        key_value_weight,
        down_all,
        adapter_up_key_value,
        cosine,
        sine,
        grad_own,
        shares,
    )
    grad_input = lax.psum_scatter(term, "tensor", scatter_dimension=0, tiled=True)[None]

    def over_tokens(low, grads):
        return jnp.einsum("tr,th->rh", low, grads, preferred_element_type=f32)

    low_rows = jnp.concatenate([hidden, (adapter_scale * factor.astype(f32)).astype(bf16).T], 0)
    low_rows = after(low_rows, term)
    mine_low = scattered_rows(low_rows, "tensor")
    row_at = lax.axis_index("tensor") * mine_low.shape[0] + jnp.arange(mine_low.shape[0])
    from_tokens = (row_at < 3 * rank)[:, None]
    zero = jnp.zeros_like(mine_low)
    mine = (
        jnp.dot(jnp.where(from_tokens, mine_low, zero), gathered, preferred_element_type=f32)
        + jnp.dot(jnp.where(from_tokens, zero, mine_low), incoming, preferred_element_type=f32)
    ).astype(bf16)
    narrow = jnp.concatenate(
        [adapter_scale * over_tokens(adapted_query, grad_query)]
        + [adapter_scale * over_tokens(adapted_key, grad_key)]
        + [adapter_scale * over_tokens(adapted_value, grad_value)]
        + [over_tokens(up_gradient, attended)],
        1,
    ).astype(bf16)
    size = mine.size
    flat = jnp.concatenate([mine.reshape(-1, 128), narrow.reshape(-1, 128)], 0)
    flat = summed_pairwise(summed_pairwise(flat, "context"), "dp")
    wide_sum = gathered_rows(flat[: size // 128].reshape(mine.shape), "tensor").astype(f32)
    narrow_sum = flat[size // 128 :].reshape(narrow.shape).astype(f32)
    q_cols, kv_cols = adapter_up_query.shape[1], adapter_up_key_value.shape[2]
    return (
        grad_input,
        wide_sum[: 3 * rank].reshape(3, rank, width),
        narrow_sum[:, :q_cols],
        jnp.stack(
            [
                narrow_sum[:, q_cols : q_cols + kv_cols],
                narrow_sum[:, q_cols + kv_cols : q_cols + 2 * kv_cols],
            ],
            0,
        ),
        narrow_sum[:, q_cols + 2 * kv_cols :],
        wide_sum[3 * rank :],
    )


def solution(mesh):
    in_specs = (
        P("dp", ("context", "tensor"), None),
        P("dp", ("context", "tensor"), None),
        P("dp", None),
        P(None, "tensor"),
        P(None, None, "tensor"),
        P("tensor", None),
        P(),
        P(None, "tensor"),
        P(None, None, "tensor"),
        P(None, "tensor"),
        P(),
    )
    out_specs = (
        P("dp", ("context", "tensor"), None),
        P(),
        P(None, "tensor"),
        P(None, None, "tensor"),
        P(None, "tensor"),
        P(),
    )
    return jax.shard_map(local, mesh=mesh, in_specs=in_specs, out_specs=out_specs, check_vma=False)
```
